256 devices in a mesh: dp: 16 (over y_lo, z), ctx: 16 (over x, y_hi, core).
Axes of the slice: x: 4, y: 4 (y_hi: 2, y_lo: 2; y = y_hi * 2 + y_lo), z: 8, core: 2. Of those that a mesh axis runs over, the one named last changes fastest.
Arguments:
- queries: bfloat16 [16, 2048, 4096], P('dp', 'ctx'), may hold values from -9 to 9
- keys: bfloat16 [16, 2048, 512], P('dp', 'ctx'), may hold values from -7 to 7
- values: bfloat16 [16, 2048, 512], P('dp', 'ctx'), may hold values from -6 to 6
- cotangent: bfloat16 [16, 2048, 4096], P('dp', 'ctx'), may hold values from -6 to 6
- live: int32 [16, 2048], P('dp', 'ctx'), may hold values from 0 to 1, as said below
- docs: int32 [16, 2048], P('dp'), may hold values from 0 to 5, never falling along the last dimension, each value on 1 to 1024 neighbouring positions
Outputs:
- attended: bfloat16 [16, 2048, 4096], P('dp', 'ctx')
- grad_queries: bfloat16 [16, 2048, 4096], P('dp', 'ctx')
- key_gradient: bfloat16 [16, 2048, 512], P('dp', 'ctx')
- value_gradient: bfloat16 [16, 2048, 512], P('dp', 'ctx')
The draws below stay inside these ranges and needn't reach their ends.
Inputs may be any that keep to these rules, and one draw needn't show every extreme that they name: `docs`: never falls along a sequence; each document spans 1 to 1024 positions and one spans exactly 1024. `live`: row 0 of every sequence is 1.
All inputs are finite; a program needn't handle non-finite values.
Results may differ from the reference program's by a relative error of at most 0.02.
Values may be sent and summed in bfloat16 or wider, within the bound.
No kernel may reach another device: no remote copies, remote signals or barrier semaphores. Data moves between devices by JAX's collectives and lax.ppermute only.
A program may use at most 64 MiB of HBM per device.

```python
import math
import jax
import jax.numpy as jnp
import numpy as np
from jax import lax

QUERY_HEADS = 32
KEY_VALUE_HEADS = 4
HEAD_SIZE = 128
TOK_DEV = 128
DOCS = 6
SEQUENCE_TOKENS = 2048
BATCH_SEQUENCES = 16
N_CTX = 16


def draw_queries(key, part):
    query_group_width = QUERY_HEADS // KEY_VALUE_HEADS
    array_shape = (BATCH_SEQUENCES, SEQUENCE_TOKENS, KEY_VALUE_HEADS, query_group_width, HEAD_SIZE)
    final_result = jnp.clip(jax.random.normal(jax.random.fold_in(key, 1), array_shape, jnp.float32), -6.0, 6.0)
    return final_result.reshape(BATCH_SEQUENCES, SEQUENCE_TOKENS, QUERY_HEADS * HEAD_SIZE).astype(jnp.bfloat16)


def draw_keys(key, part):
    array_shape = (BATCH_SEQUENCES, SEQUENCE_TOKENS, KEY_VALUE_HEADS, HEAD_SIZE)
    final_result = jnp.clip(jax.random.normal(jax.random.fold_in(key, 11), array_shape, jnp.float32), -6.0, 6.0)
    return final_result.reshape(BATCH_SEQUENCES, SEQUENCE_TOKENS, KEY_VALUE_HEADS * HEAD_SIZE).astype(jnp.bfloat16)


def draw_live(key, part):
    sequence_ids = jnp.arange(BATCH_SEQUENCES, dtype=jnp.int32)[:, None]
    cutoff = 250 + 500 * sequence_ids // max(BATCH_SEQUENCES - 1, 1)
    picks = jax.random.randint(key, (BATCH_SEQUENCES, SEQUENCE_TOKENS), 0, 1000, dtype=jnp.int32)
    counted = (picks < cutoff).astype(jnp.int32)
    first_row = jnp.arange(SEQUENCE_TOKENS, dtype=jnp.int32)[None, :] == 0
    return jnp.where(first_row, 1, counted).astype(jnp.int32)


def level_of(own_key, shape, cuts, smallest, top_value):
    level, own = 1.0, jax.random.fold_in(own_key, 6)
    for axis_at, shards_of in cuts:
        draws = jnp.exp(jax.random.uniform(jax.random.fold_in(own, axis_at), (shards_of,), jnp.float32, smallest / len(cuts), top_value / len(cuts)))
        level = level * jnp.repeat(draws, shape[axis_at] // shards_of).reshape([-1 if axis == axis_at else 1 for axis in range(len(shape))])
    return level


def profile(number_of, total, bound, lean):
    loads = [(1 << 20) // math.isqrt(grade ** lean) + 1 for grade in range(2, number_of + 1)]
    rest, given = total - bound - (number_of - 1), [1] * (number_of - 1)
    while rest > 0:
        free = [i for i in range(number_of - 1) if given[i] < bound]
        whole, remaining = sum([loads[i] for i in free]), rest
        for i in free:
            more = min(bound - given[i], max(1, remaining * loads[i] // whole), rest)
            given[i] = given[i] + more
            rest = rest - more
    return np.array([bound] + given)


def uneven_parts(own_key, count, total, limit, slope):
    if count == 2:
        one = jax.random.randint(own_key, (), max(1, total - limit), min(limit, total - 1) + 1)
        return jnp.stack([one, total - one])
    lengths = jnp.asarray(profile(count, total, limit, slope), jnp.int32)
    twos = (count - 1) // 2
    giver, taker = lengths[1:1 + 2 * twos:2], lengths[2:2 + 2 * twos:2]
    margin = jnp.minimum(giver - 1, limit - taker)
    moved = jax.random.randint(jax.random.fold_in(own_key, 1), (twos,), 0, 1 << 20) % (margin + 1)
    lengths = lengths.at[1:1 + 2 * twos:2].set(giver - moved).at[2:2 + 2 * twos:2].set(taker + moved)
    return lengths[jax.random.permutation(jax.random.fold_in(own_key, 2), count)]


def gaussian(stream_key, shape, scale, bound, pieces=(), held_as=jnp.bfloat16):
    array = scale * jax.random.normal(stream_key, shape, jnp.float32)
    if pieces:
        array = array * level_of(stream_key, shape, pieces, -0.22, 0.18)
    return jnp.clip(array, -bound, bound).astype(held_as)


def setup_inputs(seed: int = 0) -> dict:
    arg_keys = jax.random.split(jax.random.key(seed), 7)
    return {
        "queries": draw_queries(jax.random.fold_in(arg_keys[6], 71), 0),
        "keys": draw_keys(jax.random.fold_in(arg_keys[6], 71), 0),
        "values": gaussian(arg_keys[2], (BATCH_SEQUENCES, SEQUENCE_TOKENS, KEY_VALUE_HEADS * HEAD_SIZE), 1.0, 6.0, ((0, 16), (1, 16))),
        "cotangent": gaussian(arg_keys[3], (BATCH_SEQUENCES, SEQUENCE_TOKENS, QUERY_HEADS * HEAD_SIZE), 1.0, 6.0, ((0, 16), (1, 16))),
        "live": draw_live(jax.random.fold_in(arg_keys[6], 71), 0),
        "docs": jax.vmap(lambda own: jnp.searchsorted(jnp.cumsum(uneven_parts(own, DOCS, SEQUENCE_TOKENS, SEQUENCE_TOKENS // 2, 1)), jnp.arange(SEQUENCE_TOKENS), side="right"))(jax.random.split(arg_keys[5], BATCH_SEQUENCES)).reshape((BATCH_SEQUENCES, SEQUENCE_TOKENS)).astype(jnp.int32),
    }


masked_fill = -1e+30

def folded_positions():
    half_rows = TOK_DEV // 2
    offsets = jnp.arange(SEQUENCE_TOKENS, dtype=jnp.int32)
    slot_index = offsets // half_rows
    device = slot_index // 2
    piece_id = jnp.where(slot_index % 2 == 0, device, 2 * N_CTX - 1 - device)
    return piece_id * half_rows + offsets % half_rows

def one_head(query_head, grad_head, key_natural, value_natural, docs):
    score_scale = 1.0 / math.sqrt(HEAD_SIZE)
    half_rows = TOK_DEV // 2
    outs_list, rows_list = ([], [])
    key_total = jnp.zeros((SEQUENCE_TOKENS, HEAD_SIZE), query_head.dtype)
    value_total = jnp.zeros((SEQUENCE_TOKENS, HEAD_SIZE), query_head.dtype)
    for block in range(N_CTX):
        key_block = jnp.zeros((SEQUENCE_TOKENS, HEAD_SIZE), query_head.dtype)
        value_block = jnp.zeros((SEQUENCE_TOKENS, HEAD_SIZE), query_head.dtype)
        for side in range(2):
            piece_id = block if side == 0 else 2 * N_CTX - 1 - block
            row_start = block * TOK_DEV + side * half_rows
            span = (piece_id + 1) * half_rows
            query_part = query_head[row_start:row_start + half_rows]
            grad_part = grad_head[row_start:row_start + half_rows]
            key_part = key_natural[:span]
            value_part = value_natural[:span]
            query_pos = piece_id * half_rows + jnp.arange(half_rows, dtype=jnp.int32)
            key_pos = jnp.arange(span, dtype=jnp.int32)
            query_doc = docs[piece_id * half_rows:(piece_id + 1) * half_rows]
            allowed = (query_doc[:, None] == docs[:span][None, :]) & (key_pos[None, :] <= query_pos[:, None])
            scores = jnp.einsum('qjd,kd->jqk', query_part, key_part) * score_scale
            masked = jnp.where(allowed, scores, masked_fill)
            row_peak = lax.optimization_barrier(jnp.max(masked, axis=-1, keepdims=True))
            log_total = row_peak + jnp.log(lax.optimization_barrier(jnp.sum(jnp.exp(masked - row_peak), axis=-1, keepdims=True)))
            weights = jnp.where(allowed, jnp.exp(masked - log_total), 0.0)
            rounded = weights.astype(jnp.bfloat16).astype(query_head.dtype)
            attended = jnp.einsum('jqk,kd->qjd', rounded, value_part).astype(jnp.bfloat16)
            delta = jnp.transpose(lax.optimization_barrier(jnp.sum(grad_part * attended.astype(query_head.dtype), axis=-1)))[:, :, None]
            pushes = jnp.einsum('qjd,kd->jqk', grad_part, value_part)
            slopes = (weights * (pushes - delta) * score_scale).astype(jnp.bfloat16).astype(query_head.dtype)
            grad_rows = jnp.einsum('jqk,kd->qjd', slopes, key_part).astype(jnp.bfloat16)
            key_term = jnp.einsum('jqk,qjd->kd', slopes, query_part)
            value_term = jnp.einsum('jqk,qjd->kd', rounded, grad_part)
            key_block = key_block.at[:span].add(key_term)
            value_block = value_block.at[:span].add(value_term)
            outs_list.append(attended)
            rows_list.append(grad_rows)
        key_total = key_total + lax.optimization_barrier(key_block.astype(jnp.bfloat16)).astype(query_head.dtype)
        value_total = value_total + lax.optimization_barrier(value_block.astype(jnp.bfloat16)).astype(query_head.dtype)
    return (jnp.concatenate(outs_list, axis=0), jnp.concatenate(rows_list, axis=0), key_total.astype(jnp.bfloat16), value_total.astype(jnp.bfloat16))

def one_sequence(queries, keys, values, cotangent, live, docs, loss_ratio):
    query_group_width = QUERY_HEADS // KEY_VALUE_HEADS
    positions = folded_positions()
    inverse = jnp.zeros((SEQUENCE_TOKENS,), jnp.int32).at[positions].set(jnp.arange(SEQUENCE_TOKENS, dtype=jnp.int32))
    work_type = loss_ratio.dtype
    output_gradient = (cotangent.astype(work_type) * live.astype(work_type)[:, None] * loss_ratio).astype(jnp.bfloat16)
    query_heads = jnp.transpose(queries.reshape(SEQUENCE_TOKENS, KEY_VALUE_HEADS, query_group_width, HEAD_SIZE).astype(work_type), (1, 0, 2, 3))
    grad_heads = jnp.transpose(output_gradient.reshape(SEQUENCE_TOKENS, KEY_VALUE_HEADS, query_group_width, HEAD_SIZE).astype(work_type), (1, 0, 2, 3))
    key_heads = jnp.transpose(jnp.take(keys, inverse, axis=0).reshape(SEQUENCE_TOKENS, KEY_VALUE_HEADS, HEAD_SIZE).astype(work_type), (1, 0, 2))
    value_heads = jnp.transpose(jnp.take(values, inverse, axis=0).reshape(SEQUENCE_TOKENS, KEY_VALUE_HEADS, HEAD_SIZE).astype(work_type), (1, 0, 2))

    def per_head(operands):
        return one_head(operands[0], operands[1], operands[2], operands[3], docs)
    attended, grad_rows, key_sum, value_sum = lax.map(per_head, (query_heads, grad_heads, key_heads, value_heads))
    attended_all = jnp.transpose(attended, (1, 0, 2, 3)).reshape(SEQUENCE_TOKENS, QUERY_HEADS * HEAD_SIZE)
    grad_queries = jnp.transpose(grad_rows, (1, 0, 2, 3)).reshape(SEQUENCE_TOKENS, QUERY_HEADS * HEAD_SIZE)
    key_gradient = jnp.take(jnp.transpose(key_sum, (1, 0, 2)), positions, axis=0).reshape(SEQUENCE_TOKENS, KEY_VALUE_HEADS * HEAD_SIZE)
    value_gradient = jnp.take(jnp.transpose(value_sum, (1, 0, 2)), positions, axis=0).reshape(SEQUENCE_TOKENS, KEY_VALUE_HEADS * HEAD_SIZE)
    return (attended_all, grad_queries, key_gradient, value_gradient)

def reference(queries, keys, values, cotangent, live, docs):
    live_count = jnp.sum(live).astype(jnp.float32)
    loss_ratio = float(BATCH_SEQUENCES * SEQUENCE_TOKENS) / live_count

    def per_sequence(operands):
        return one_sequence(operands[0], operands[1], operands[2], operands[3], operands[4], operands[5], loss_ratio)
    return lax.map(per_sequence, (queries, keys, values, cotangent, live, docs))
```

```python
from functools import partial
import math

import jax
import jax.numpy as jnp
from jax import lax
from jax.experimental import pallas as pl
from jax.experimental.pallas import tpu as pltpu
from jax.sharding import PartitionSpec as P

HEAD = 128
BLOCK = 128
TILE = 256
GROUPS = 2
FOLD = 8
ROWS = FOLD * BLOCK
MASKED = -1e30
SCALE = 1.0 / math.sqrt(HEAD)
SCALE_LOG2E = SCALE * math.log2(math.e)

NT = (((1,), (1,)), ((), ()))
NN = (((1,), (0,)), ((), ()))


def dot(a, b, dims=NN):
    return lax.dot_general(a, b, dims, preferred_element_type=jnp.float32)


def attention_kernel(
    info_ref,
    bounds_ref,
    q_own,
    q_sib,
    c_own,
    c_sib,
    *refs,
):
    chips = 8
    chunks = refs[:chips]
    o_own, o_sib, dq_own, dq_sib = refs[chips : chips + 4]
    terms = refs[chips + 4 : 2 * chips + 4]
    (
        k_nat,
        v_nat,
        s_ref,
        p_ref,
        q_ref,
        do_ref,
        qt_ref,
        dot_ref,
        m_ref,
        l_ref,
        o_ref,
        dq_ref,
        dkt_ref,
        dvt_ref,
    ) = refs[2 * chips + 4 :]

    for group in range(GROUPS):
        k_nat[group, 0:BLOCK, :] = jnp.zeros((BLOCK, HEAD), jnp.bfloat16)
        v_nat[group, 0:BLOCK, :] = jnp.zeros((BLOCK, HEAD), jnp.bfloat16)
    for at, chunk in enumerate(chunks):
        low = info_ref[4 + at]
        for half in range(2):
            block = low if half == 0 else 15 - low
            place = pl.ds(pl.multiple_of((block + 1) * BLOCK, BLOCK), BLOCK)
            rows = slice(half * BLOCK, (half + 1) * BLOCK)
            for group in range(GROUPS):
                k_nat[group, place, :] = chunk[rows, group * HEAD : (group + 1) * HEAD]
                v_nat[group, place, :] = chunk[
                    rows, (GROUPS + group) * HEAD : (GROUPS + group + 1) * HEAD
                ]

    for group in range(GROUPS):
        dkt_ref[...] = jnp.zeros_like(dkt_ref)
        dvt_ref[...] = jnp.zeros_like(dvt_ref)
        for half in range(2):
            tiles = info_ref[half]
            end = info_ref[2 + half]
            rows = slice(half * 64, half * 64 + 64)
            low_bound = bounds_ref[half * BLOCK : (half + 1) * BLOCK, 0:1]
            own_pos = bounds_ref[half * BLOCK : (half + 1) * BLOCK, 1:2]
            live = bounds_ref[half * BLOCK : (half + 1) * BLOCK, 2:3].astype(jnp.float32)

            def columns(head):
                return slice((group * FOLD + head) * HEAD, (group * FOLD + head + 1) * HEAD)

            for head in range(FOLD):
                q_ref[head * BLOCK : head * BLOCK + 64, :] = q_own[rows, columns(head)]
                q_ref[head * BLOCK + 64 : (head + 1) * BLOCK, :] = q_sib[rows, columns(head)]
            m_ref[...] = jnp.full_like(m_ref, MASKED)
            l_ref[...] = jnp.zeros_like(l_ref)
            o_ref[...] = jnp.zeros_like(o_ref)
            dq_ref[...] = jnp.zeros_like(dq_ref)

            def key_rows(j):
                return pl.ds(pl.multiple_of(end - TILE * (j + 1) + BLOCK, BLOCK), TILE)

            def tile_columns(j):
                return pl.ds(pl.multiple_of(j * TILE, TILE), TILE)

            def score_tile(j, _):
                first = end - TILE * (j + 1)
                key_pos = first + lax.broadcasted_iota(jnp.int32, (BLOCK, TILE), 1)
                bias = jnp.where((key_pos >= low_bound) & (key_pos <= own_pos), 0.0, MASKED)
                scores = dot(q_ref[...], k_nat[group, key_rows(j), :], NT)
                scores = (
                    scores.reshape(FOLD, BLOCK, TILE) * SCALE_LOG2E + bias[None]
                ).reshape(ROWS, TILE)
                s_ref[:, tile_columns(j)] = scores
                m_ref[...] = jnp.maximum(
                    m_ref[...], jnp.maximum(scores[:, :HEAD], scores[:, HEAD:])
                )
                return 0

            lax.fori_loop(0, tiles, score_tile, 0)
            m_ref[...] = jnp.broadcast_to(
                jnp.max(m_ref[...], axis=1, keepdims=True), (ROWS, HEAD)
            )

            def weight_tile(j, _):
                peak = m_ref[...]
                scores = s_ref[:, tile_columns(j)]
                left = jnp.exp2(scores[:, :HEAD] - peak)
                right = jnp.exp2(scores[:, HEAD:] - peak)
                l_ref[...] += left + right
                weights = jnp.concatenate([left, right], axis=1).astype(jnp.bfloat16)
                p_ref[:, tile_columns(j)] = weights
                o_ref[...] += dot(weights, v_nat[group, key_rows(j), :])
                return 0

            lax.fori_loop(0, tiles, weight_tile, 0)
            for head in range(FOLD):
                span = slice(head * BLOCK, (head + 1) * BLOCK)
                inverse = 1.0 / jnp.sum(l_ref[span, :], axis=1, keepdims=True)
                out = (o_ref[span, :] * inverse).astype(jnp.bfloat16)
                o_own[rows, columns(head)] = out[:64]
                o_sib[rows, columns(head)] = out[64:]
                cot = jnp.concatenate(
                    [c_own[rows, columns(head)], c_sib[rows, columns(head)]], axis=0
                )
                grad = (cot.astype(jnp.float32) * (live * inverse)).astype(jnp.bfloat16)
                do_ref[span, :] = grad
                m_ref[span, :] = jnp.broadcast_to(
                    jnp.sum(
                        grad.astype(jnp.float32) * out.astype(jnp.float32), axis=1, keepdims=True
                    ),
                    (BLOCK, HEAD),
                )
            qt_ref[...] = q_ref[...].T
            dot_ref[...] = do_ref[...].T

            def gradient_tile(j, _):
                delta = m_ref[...]
                pushes = dot(do_ref[...], v_nat[group, key_rows(j), :], NT)
                weights = p_ref[:, tile_columns(j)]
                wide = weights.astype(jnp.float32)
                slopes = jnp.concatenate(
                    [
                        wide[:, :HEAD] * (pushes[:, :HEAD] - delta),
                        wide[:, HEAD:] * (pushes[:, HEAD:] - delta),
                    ],
                    axis=1,
                ).astype(jnp.bfloat16)
                dq_ref[...] += dot(slopes, k_nat[group, key_rows(j), :])
                dkt_ref[:, key_rows(j)] += dot(qt_ref[...], slopes)
                dvt_ref[:, key_rows(j)] += dot(dot_ref[...], weights)
                return 0

            lax.fori_loop(0, tiles, gradient_tile, 0)
            for head in range(FOLD):
                span = slice(head * BLOCK, (head + 1) * BLOCK)
                out = (dq_ref[span, :] * SCALE).astype(jnp.bfloat16)
                dq_own[rows, columns(head)] = out[:64]
                dq_sib[rows, columns(head)] = out[64:]
        for at, term in enumerate(terms):
            low = info_ref[4 + at]
            for half in range(2):
                block = low if half == 0 else 15 - low
                place = pl.ds(pl.multiple_of((block + 1) * BLOCK, BLOCK), BLOCK)
                lanes = slice(half * BLOCK, (half + 1) * BLOCK)
                term[group * HEAD : (group + 1) * HEAD, lanes] = (
                    dkt_ref[:, place] * SCALE
                ).astype(jnp.bfloat16)
                term[(GROUPS + group) * HEAD : (GROUPS + group + 1) * HEAD, lanes] = dvt_ref[
                    :, place
                ].astype(jnp.bfloat16)


def attention(info, bounds, q_own, q_sib, c_own, c_sib, chunks, interpret=False):
    vmem = pl.BlockSpec(memory_space=pltpu.VMEM)
    half_rows = jax.ShapeDtypeStruct((128, GROUPS * FOLD * HEAD), jnp.bfloat16)
    term = jax.ShapeDtypeStruct((2 * GROUPS * HEAD, 2 * BLOCK), jnp.bfloat16)
    padded = 2048 + BLOCK
    most = 5
    return pl.pallas_call(
        attention_kernel,
        out_shape=(half_rows,) * 4 + (term,) * 8,
        in_specs=[pl.BlockSpec(memory_space=pltpu.SMEM)] + [vmem] * 13,
        out_specs=(vmem,) * 12,
        scratch_shapes=[
            pltpu.VMEM((GROUPS, padded, HEAD), jnp.bfloat16),
            pltpu.VMEM((GROUPS, padded, HEAD), jnp.bfloat16),
            pltpu.VMEM((ROWS, most * TILE), jnp.float32),
            pltpu.VMEM((ROWS, most * TILE), jnp.bfloat16),
            pltpu.VMEM((ROWS, HEAD), jnp.bfloat16),
            pltpu.VMEM((ROWS, HEAD), jnp.bfloat16),
            pltpu.VMEM((HEAD, ROWS), jnp.bfloat16),
            pltpu.VMEM((HEAD, ROWS), jnp.bfloat16),
            pltpu.VMEM((ROWS, HEAD), jnp.float32),
            pltpu.VMEM((ROWS, HEAD), jnp.float32),
            pltpu.VMEM((ROWS, HEAD), jnp.float32),
            pltpu.VMEM((ROWS, HEAD), jnp.float32),
            pltpu.VMEM((HEAD, padded), jnp.float32),
            pltpu.VMEM((HEAD, padded), jnp.float32),
        ],
        compiler_params=pltpu.CompilerParams(vmem_limit_bytes=40 * 1024 * 1024),
        cost_estimate=pl.CostEstimate(
            flops=6_000_000_000, bytes_accessed=8_000_000, transcendentals=4_000_000
        ),
        interpret=interpret,
    )(info, bounds, q_own, q_sib, c_own, c_sib, *chunks)


def on_device(queries, keys, values, cotangent, live, docs):
    me = lax.axis_index("ctx")
    core = me % 2
    chip = me // 2
    line, side = chip // 2, chip % 2

    def move(shift):
        return [(i, (i + shift) % 16) for i in range(16)]

    def swap(bit):
        return [(i, i ^ bit) for i in range(16)]

    def to_right(a):
        return lax.ppermute(a, "ctx", move(4))

    def to_left(a):
        return lax.ppermute(a, "ctx", move(-4))

    def to_side(a):
        return lax.ppermute(a, "ctx", swap(2))

    def to_core(a):
        return lax.ppermute(a, "ctx", swap(1))

    def part(a, which, width):
        return lax.dynamic_slice_in_dim(a, which * width, width, 1)

    kv_width = GROUPS * HEAD
    kv_send = jnp.concatenate(
        [part(keys[0], 1 - core, kv_width), part(values[0], 1 - core, kv_width)], axis=1
    )
    kv_keep = jnp.concatenate(
        [part(keys[0], core, kv_width), part(values[0], core, kv_width)], axis=1
    )
    kv_got = to_core(kv_send)
    first = jnp.where(core == 0, kv_keep, kv_got)
    second = jnp.where(core == 0, kv_got, kv_keep)
    mine = jnp.concatenate([first[:64], second[:64], second[64:], first[64:]], axis=0)

    from_left = to_right(mine)
    from_right = to_left(mine)
    beside = to_side(mine)
    beside_left = to_right(beside)
    beside_right = to_left(beside)
    opposite = to_right(from_left)
    beside_opposite = to_left(beside_right)
    chunks = (
        mine,
        beside,
        from_right,
        beside_right,
        from_left,
        beside_left,
        opposite,
        beside_opposite,
    )

    q_width = GROUPS * FOLD * HEAD
    q_own, c_own = part(queries[0], core, q_width), part(cotangent[0], core, q_width)
    q_sib = to_core(part(queries[0], 1 - core, q_width))
    c_sib = to_core(part(cotangent[0], 1 - core, q_width))

    own_live = live[0]
    sib_live = to_core(own_live)
    count = jnp.broadcast_to(
        jnp.sum(own_live + sib_live).astype(jnp.float32), (8, 128)
    )
    for bit in (2, 4, 8):
        count = count + lax.ppermute(count, "ctx", swap(bit))
    for bit in (1, 2, 4, 8):
        count = count + lax.ppermute(count, "dp", swap(bit))
    loss_ratio = 32768.0 / count[0, 0]

    offsets = jnp.arange(64, dtype=jnp.int32)
    pieces = [2 * chip + core, 2 * chip + 1 - core, 31 - 2 * chip - core, 30 - 2 * chip + core]
    own_pos = jnp.concatenate([piece * 64 + offsets for piece in pieces])
    row_docs = jnp.concatenate(
        [lax.dynamic_slice_in_dim(docs[0], piece * 64, 64) for piece in pieces]
    )
    low_bound = jnp.sum((docs[0][None, :] < row_docs[:, None]).astype(jnp.int32), axis=1)
    row_live = jnp.concatenate([own_live[:64], sib_live[:64], own_live[64:], sib_live[64:]])
    bounds = jnp.stack([low_bound, own_pos, row_live], axis=1)
    ends = jnp.stack([(chip + 1) * BLOCK, (16 - chip) * BLOCK])
    lows = jnp.stack([jnp.min(low_bound[:128]), jnp.min(low_bound[128:])])
    tiles = (ends - lows + TILE - 1) // TILE
    lines = [line, line, (line + 1) % 4, (line + 1) % 4, (line + 3) % 4, (line + 3) % 4]
    lines += [(line + 2) % 4] * 2
    sides = [side, 1 - side] * 4
    lows_of = jnp.stack([2 * a + b for a, b in zip(lines, sides)])
    info = jnp.concatenate([tiles, ends, lows_of]).astype(jnp.int32)

    results = attention(info, bounds, q_own, q_sib, c_own, c_sib, chunks)
    o_own, o_sib, dq_own, dq_sib = results[:4]
    t_mine, t_beside, t_right, t_beside_right, t_left, t_beside_left, t_opp, t_beside_opp = (
        results[4:]
    )

    def add(*terms):
        return sum(t.astype(jnp.float32) for t in terms).astype(jnp.bfloat16)

    opp_via_right = to_right(t_opp)
    opp_via_left = to_left(t_beside_opp)
    got_beside_1 = to_right(t_beside_right)
    got_mine_1 = to_left(t_left)
    got_mine_2 = to_right(add(t_right, opp_via_right))
    got_beside_2 = to_left(add(t_beside_left, opp_via_left))
    got_side = to_side(add(t_beside, got_beside_1, got_beside_2))
    total = add(t_mine, got_mine_1, got_mine_2, got_side)

    o_got, dq_got = to_core(o_sib), to_core(dq_sib)

    def join(own, got, width):
        low = jnp.where(core == 0, own, got)
        high = jnp.where(core == 0, got, own)
        return jnp.concatenate([low, high], axis=1)

    attended = join(o_own, o_got, q_width)[None]
    grad_queries = (join(dq_own, dq_got, q_width).astype(jnp.float32) * loss_ratio).astype(
        jnp.bfloat16
    )[None]

    token_rows = total.T
    rows_0 = jnp.concatenate([token_rows[:64], token_rows[192:]], axis=0)
    rows_1 = token_rows[64:192]
    kept = jnp.where(core == 0, rows_0, rows_1)
    got = to_core(jnp.where(core == 0, rows_1, rows_0))

    def gradient(at):
        columns = slice(at * kv_width, (at + 1) * kv_width)
        joined = join(kept[:, columns], got[:, columns], kv_width)
        return (joined.astype(jnp.float32) * loss_ratio).astype(jnp.bfloat16)[None]

    return attended, grad_queries, gradient(0), gradient(1)


def solution(mesh):
    rows = P("dp", "ctx", None)
    return jax.shard_map(
        on_device,
        mesh=mesh,
        in_specs=(rows, rows, rows, rows, P("dp", "ctx"), P("dp", None)),
        out_specs=(rows, rows, rows, rows),
        check_vma=False,
    )
```

```python
from functools import partial
import math

import jax
import jax.numpy as jnp
from jax import lax
from jax.experimental import pallas as pl
from jax.experimental.pallas import tpu as pltpu
from jax.sharding import PartitionSpec as P

HEAD = 128
BLOCK = 128
TILE = 256
GROUPS = 2
FOLD = 8
ROWS = FOLD * BLOCK
MASKED = -1e30
SCALE = 1.0 / math.sqrt(HEAD)
SCALE_LOG2E = SCALE * math.log2(math.e)

TERM_ROWS = 2 * GROUPS * HEAD + 16
DIGIT = 32

NT = (((1,), (1,)), ((), ()))
NN = (((1,), (0,)), ((), ()))


def dot(a, b, dims=NN):
    return lax.dot_general(a, b, dims, preferred_element_type=jnp.float32)


def attention_kernel(
    info_ref,
    bounds_ref,
    q_own,
    q_sib,
    c_own,
    c_sib,
    *refs,
):
    chips = 8
    chunks = refs[:chips]
    o_own, o_sib, dq_own, dq_sib = refs[chips : chips + 4]
    terms = refs[chips + 4 : 2 * chips + 4]
    (
        k_nat,
        v_nat,
        s_ref,
        p_ref,
        q_ref,
        do_ref,
        qt_ref,
        dot_ref,
        m_ref,
        l_ref,
        o_ref,
        dq_ref,
        dkt_ref,
        dvt_ref,
    ) = refs[2 * chips + 4 :]

    for group in range(GROUPS):
        k_nat[group, 0:BLOCK, :] = jnp.zeros((BLOCK, HEAD), jnp.bfloat16)
        v_nat[group, 0:BLOCK, :] = jnp.zeros((BLOCK, HEAD), jnp.bfloat16)
    for at, chunk in enumerate(chunks):
        low = info_ref[4 + at]
        for half in range(2):
            block = low if half == 0 else 15 - low
            place = pl.ds(pl.multiple_of((block + 1) * BLOCK, BLOCK), BLOCK)
            rows = slice(half * BLOCK, (half + 1) * BLOCK)
            for group in range(GROUPS):
                k_nat[group, place, :] = chunk[rows, group * HEAD : (group + 1) * HEAD]
                v_nat[group, place, :] = chunk[
                    rows, (GROUPS + group) * HEAD : (GROUPS + group + 1) * HEAD
                ]

    for group in range(GROUPS):
        dkt_ref[...] = jnp.zeros_like(dkt_ref)
        dvt_ref[...] = jnp.zeros_like(dvt_ref)
        for half in range(2):
            tiles = info_ref[half]
            end = info_ref[2 + half]
            rows = slice(half * 64, half * 64 + 64)
            low_bound = bounds_ref[half * BLOCK : (half + 1) * BLOCK, 0:1]
            own_pos = bounds_ref[half * BLOCK : (half + 1) * BLOCK, 1:2]
            live = bounds_ref[half * BLOCK : (half + 1) * BLOCK, 2:3].astype(jnp.float32)

            def columns(head):
                return slice((group * FOLD + head) * HEAD, (group * FOLD + head + 1) * HEAD)

            for head in range(FOLD):
                q_ref[head * BLOCK : head * BLOCK + 64, :] = q_own[rows, columns(head)]
                q_ref[head * BLOCK + 64 : (head + 1) * BLOCK, :] = q_sib[rows, columns(head)]
            m_ref[...] = jnp.full_like(m_ref, MASKED)
            l_ref[...] = jnp.zeros_like(l_ref)
            o_ref[...] = jnp.zeros_like(o_ref)
            dq_ref[...] = jnp.zeros_like(dq_ref)

            def key_rows(j):
                return pl.ds(pl.multiple_of(end - TILE * (j + 1) + BLOCK, BLOCK), TILE)

            def tile_columns(j):
                return pl.ds(pl.multiple_of(j * TILE, TILE), TILE)

            def score_tile(j, _):
                first = end - TILE * (j + 1)
                key_pos = first + lax.broadcasted_iota(jnp.int32, (BLOCK, TILE), 1)
                bias = jnp.where((key_pos >= low_bound) & (key_pos <= own_pos), 0.0, MASKED)
                scores = dot(q_ref[...], k_nat[group, key_rows(j), :], NT)
                scores = (
                    scores.reshape(FOLD, BLOCK, TILE) * SCALE_LOG2E + bias[None]
                ).reshape(ROWS, TILE)
                s_ref[:, tile_columns(j)] = scores
                m_ref[...] = jnp.maximum(
                    m_ref[...], jnp.maximum(scores[:, :HEAD], scores[:, HEAD:])
                )
                return 0

            lax.fori_loop(0, tiles, score_tile, 0)
            m_ref[...] = jnp.broadcast_to(
                jnp.max(m_ref[...], axis=1, keepdims=True), (ROWS, HEAD)
            )

            def weight_tile(j, _):
                peak = m_ref[...]
                scores = s_ref[:, tile_columns(j)]
                left = jnp.exp2(scores[:, :HEAD] - peak)
                right = jnp.exp2(scores[:, HEAD:] - peak)
                l_ref[...] += left + right
                weights = jnp.concatenate([left, right], axis=1).astype(jnp.bfloat16)
                p_ref[:, tile_columns(j)] = weights
                o_ref[...] += dot(weights, v_nat[group, key_rows(j), :])
                return 0

            lax.fori_loop(0, tiles, weight_tile, 0)
            for head in range(FOLD):
                span = slice(head * BLOCK, (head + 1) * BLOCK)
                inverse = 1.0 / jnp.sum(l_ref[span, :], axis=1, keepdims=True)
                out = (o_ref[span, :] * inverse).astype(jnp.bfloat16)
                o_own[rows, columns(head)] = out[:64]
                o_sib[rows, columns(head)] = out[64:]
                cot = jnp.concatenate(
                    [c_own[rows, columns(head)], c_sib[rows, columns(head)]], axis=0
                )
                grad = (cot.astype(jnp.float32) * (live * inverse)).astype(jnp.bfloat16)
                do_ref[span, :] = grad
                m_ref[span, :] = jnp.broadcast_to(
                    jnp.sum(
                        grad.astype(jnp.float32) * out.astype(jnp.float32), axis=1, keepdims=True
                    ),
                    (BLOCK, HEAD),
                )
            qt_ref[...] = q_ref[...].T
            dot_ref[...] = do_ref[...].T

            def gradient_tile(j, _):
                delta = m_ref[...]
                pushes = dot(do_ref[...], v_nat[group, key_rows(j), :], NT)
                weights = p_ref[:, tile_columns(j)]
                wide = weights.astype(jnp.float32)
                slopes = jnp.concatenate(
                    [
                        wide[:, :HEAD] * (pushes[:, :HEAD] - delta),
                        wide[:, HEAD:] * (pushes[:, HEAD:] - delta),
                    ],
                    axis=1,
                ).astype(jnp.bfloat16)
                dq_ref[...] += dot(slopes, k_nat[group, key_rows(j), :])
                dkt_ref[:, key_rows(j)] += dot(qt_ref[...], slopes)
                dvt_ref[:, key_rows(j)] += dot(dot_ref[...], weights)
                return 0

            lax.fori_loop(0, tiles, gradient_tile, 0)
            for head in range(FOLD):
                span = slice(head * BLOCK, (head + 1) * BLOCK)
                out = (dq_ref[span, :] * SCALE).astype(jnp.bfloat16)
                dq_own[rows, columns(head)] = out[:64]
                dq_sib[rows, columns(head)] = out[64:]
        for at, term in enumerate(terms):
            low = info_ref[4 + at]
            if group == 0:
                digit_row = lax.broadcasted_iota(jnp.int32, (16, 2 * BLOCK), 0)
                digits = jnp.zeros((16, 2 * BLOCK), jnp.float32)
                for place in range(3):
                    digits = jnp.where(
                        digit_row == place, info_ref[12 + place].astype(jnp.float32), digits
                    )
                term[2 * GROUPS * HEAD :, :] = digits.astype(jnp.bfloat16)
            for half in range(2):
                block = low if half == 0 else 15 - low
                place = pl.ds(pl.multiple_of((block + 1) * BLOCK, BLOCK), BLOCK)
                lanes = slice(half * BLOCK, (half + 1) * BLOCK)
                term[group * HEAD : (group + 1) * HEAD, lanes] = (
                    dkt_ref[:, place] * SCALE
                ).astype(jnp.bfloat16)
                term[(GROUPS + group) * HEAD : (GROUPS + group + 1) * HEAD, lanes] = dvt_ref[
                    :, place
                ].astype(jnp.bfloat16)


def attention(info, bounds, q_own, q_sib, c_own, c_sib, chunks, interpret=False):
    vmem = pl.BlockSpec(memory_space=pltpu.VMEM)
    half_rows = jax.ShapeDtypeStruct((128, GROUPS * FOLD * HEAD), jnp.bfloat16)
    term = jax.ShapeDtypeStruct((TERM_ROWS, 2 * BLOCK), jnp.bfloat16)
    padded = 2048 + BLOCK
    most = 5
    return pl.pallas_call(
        attention_kernel,
        out_shape=(half_rows,) * 4 + (term,) * 8,
        in_specs=[pl.BlockSpec(memory_space=pltpu.SMEM)] + [vmem] * 13,
        out_specs=(vmem,) * 12,
        scratch_shapes=[
            pltpu.VMEM((GROUPS, padded, HEAD), jnp.bfloat16),
            pltpu.VMEM((GROUPS, padded, HEAD), jnp.bfloat16),
            pltpu.VMEM((ROWS, most * TILE), jnp.float32),
            pltpu.VMEM((ROWS, most * TILE), jnp.bfloat16),
            pltpu.VMEM((ROWS, HEAD), jnp.bfloat16),
            pltpu.VMEM((ROWS, HEAD), jnp.bfloat16),
            pltpu.VMEM((HEAD, ROWS), jnp.bfloat16),
            pltpu.VMEM((HEAD, ROWS), jnp.bfloat16),
            pltpu.VMEM((ROWS, HEAD), jnp.float32),
            pltpu.VMEM((ROWS, HEAD), jnp.float32),
            pltpu.VMEM((ROWS, HEAD), jnp.float32),
            pltpu.VMEM((ROWS, HEAD), jnp.float32),
            pltpu.VMEM((HEAD, padded), jnp.float32),
            pltpu.VMEM((HEAD, padded), jnp.float32),
        ],
        compiler_params=pltpu.CompilerParams(vmem_limit_bytes=20 * 1024 * 1024),
        cost_estimate=pl.CostEstimate(
            flops=6_000_000_000, bytes_accessed=8_000_000, transcendentals=4_000_000
        ),
        interpret=interpret,
    )(info, bounds, q_own, q_sib, c_own, c_sib, *chunks)


def closing_kernel(info_ref, *refs):
    terms, (kept, sent, ratio) = refs[:4], refs[4:]
    total = sum(term[...].astype(jnp.float32) for term in terms)
    width = 2 * GROUPS * HEAD
    digits = total[width : width + 8, :HEAD]
    count = digits[0:1] + DIGIT * (digits[1:2] + DIGIT * digits[2:3])
    ratio_row = 32768.0 / count
    ratio[...] = jnp.broadcast_to(ratio_row, (8, HEAD))
    rows = (total[:width] * ratio_row[:, :1]).T
    outer = jnp.concatenate([rows[:64], rows[192:]], axis=0).astype(jnp.bfloat16)
    inner = rows[64:192].astype(jnp.bfloat16)
    first = info_ref[0] == 0
    kept[...] = jnp.where(first, outer, inner)
    sent[...] = jnp.where(first, inner, outer)


def closing(info, terms):
    vmem = pl.BlockSpec(memory_space=pltpu.VMEM)
    rows = jax.ShapeDtypeStruct((BLOCK, 2 * GROUPS * HEAD), jnp.bfloat16)
    return pl.pallas_call(
        closing_kernel,
        out_shape=(rows, rows, jax.ShapeDtypeStruct((8, HEAD), jnp.float32)),
        in_specs=[pl.BlockSpec(memory_space=pltpu.SMEM)] + [vmem] * 4,
        out_specs=(vmem,) * 3,
        compiler_params=pltpu.CompilerParams(vmem_limit_bytes=8 * 1024 * 1024),
        cost_estimate=pl.CostEstimate(flops=1_000_000, bytes_accessed=1_000_000, transcendentals=0),
    )(info, *terms)


def on_device(queries, keys, values, cotangent, live, docs):
    me = lax.axis_index("ctx")
    core = me % 2
    chip = me // 2
    line, side = chip // 2, chip % 2

    def move(shift):
        return [(i, (i + shift) % 16) for i in range(16)]

    def swap(bit):
        return [(i, i ^ bit) for i in range(16)]

    def to_right(a):
        return lax.ppermute(a, "ctx", move(4))

    def to_left(a):
        return lax.ppermute(a, "ctx", move(-4))

    def to_side(a):
        return lax.ppermute(a, "ctx", swap(2))

    def to_core(a):
        return lax.ppermute(a, "ctx", swap(1))

    def part(a, which, width):
        return lax.dynamic_slice_in_dim(a, which * width, width, 1)

    kv_width = GROUPS * HEAD
    kv_send = jnp.concatenate(
        [part(keys[0], 1 - core, kv_width), part(values[0], 1 - core, kv_width)], axis=1
    )
    kv_keep = jnp.concatenate(
        [part(keys[0], core, kv_width), part(values[0], core, kv_width)], axis=1
    )
    kv_got = to_core(kv_send)
    first = jnp.where(core == 0, kv_keep, kv_got)
    second = jnp.where(core == 0, kv_got, kv_keep)
    mine = jnp.concatenate([first[:64], second[:64], second[64:], first[64:]], axis=0)

    from_left = to_right(mine)
    from_right = to_left(mine)
    beside = to_side(mine)
    beside_left = to_right(beside)
    beside_right = to_left(beside)
    opposite = to_right(from_left)
    beside_opposite = to_left(beside_right)
    chunks = (
        mine,
        beside,
        from_right,
        beside_right,
        from_left,
        beside_left,
        opposite,
        beside_opposite,
    )

    own_live = live[0]
    sib_live = to_core(own_live)
    count = jnp.broadcast_to(jnp.sum(own_live + sib_live).astype(jnp.float32), (8, 128))
    for bit in (1, 2):
        count = count + lax.ppermute(count, "dp", swap(bit))
    queries, cotangent, count, _ = lax.optimization_barrier((queries, cotangent, count, beside))
    for bit in (4, 8):
        count = count + lax.ppermute(count, "dp", swap(bit))
    chip_count = count[0, 0].astype(jnp.int32)

    q_width = GROUPS * FOLD * HEAD
    q_sib = to_core(part(queries[0], 1 - core, q_width))
    c_sib = to_core(part(cotangent[0], 1 - core, q_width))
    q_own, c_own = part(queries[0], core, q_width), part(cotangent[0], core, q_width)

    offsets = jnp.arange(64, dtype=jnp.int32)
    pieces = [2 * chip + core, 2 * chip + 1 - core, 31 - 2 * chip - core, 30 - 2 * chip + core]
    own_pos = jnp.concatenate([piece * 64 + offsets for piece in pieces])
    row_docs = jnp.concatenate(
        [lax.dynamic_slice_in_dim(docs[0], piece * 64, 64) for piece in pieces]
    )
    low_bound = jnp.sum((docs[0][None, :] < row_docs[:, None]).astype(jnp.int32), axis=1)
    row_live = jnp.concatenate([own_live[:64], sib_live[:64], own_live[64:], sib_live[64:]])
    bounds = jnp.stack([low_bound, own_pos, row_live], axis=1)
    ends = jnp.stack([(chip + 1) * BLOCK, (16 - chip) * BLOCK])
    lows = jnp.stack([jnp.min(low_bound[:128]), jnp.min(low_bound[128:])])
    tiles = (ends - lows + TILE - 1) // TILE
    lines = [line, line, (line + 1) % 4, (line + 1) % 4, (line + 3) % 4, (line + 3) % 4]
    lines += [(line + 2) % 4] * 2
    sides = [side, 1 - side] * 4
    lows_of = jnp.stack([2 * a + b for a, b in zip(lines, sides)])
    digits = jnp.stack(
        [chip_count % DIGIT, chip_count // DIGIT % DIGIT, chip_count // (DIGIT * DIGIT)]
    )
    info = jnp.concatenate([tiles, ends, lows_of, digits]).astype(jnp.int32)

    results = attention(info, bounds, q_own, q_sib, c_own, c_sib, chunks)
    o_own, o_sib, dq_own, dq_sib = results[:4]
    t_mine, t_beside, t_right, t_beside_right, t_left, t_beside_left, t_opp, t_beside_opp = (
        results[4:]
    )

    def add(*terms):
        return sum(t.astype(jnp.float32) for t in terms).astype(jnp.bfloat16)

    opp_via_right = to_right(t_opp)
    opp_via_left = to_left(t_beside_opp)
    got_beside_1 = to_right(t_beside_right)
    got_mine_1 = to_left(t_left)
    got_mine_2 = to_right(add(t_right, opp_via_right))
    got_beside_2 = to_left(add(t_beside_left, opp_via_left))
    got_side = to_side(add(t_beside, got_beside_1, got_beside_2))
    kept, sent, ratio = closing(
        core.reshape(1).astype(jnp.int32), (t_mine, got_mine_1, got_mine_2, got_side)
    )
    got = to_core(sent)

    o_got, dq_got = to_core(o_sib), to_core(dq_sib)

    def join(own, got, width):
        low = jnp.where(core == 0, own, got)
        high = jnp.where(core == 0, got, own)
        return jnp.concatenate([low, high], axis=1)

    attended = join(o_own, o_got, q_width)[None]
    grad_queries = (join(dq_own, dq_got, q_width).astype(jnp.float32) * ratio[0, 0]).astype(
        jnp.bfloat16
    )[None]

    def gradient(at):
        columns = slice(at * kv_width, (at + 1) * kv_width)
        return join(kept[:, columns], got[:, columns], kv_width)[None]

    return attended, grad_queries, gradient(0), gradient(1)


def solution(mesh):
    rows = P("dp", "ctx", None)
    return jax.shard_map(
        on_device,
        mesh=mesh,
        in_specs=(rows, rows, rows, rows, P("dp", "ctx"), P("dp", None)),
        out_specs=(rows, rows, rows, rows),
        check_vma=False,
    )
```

```python
from functools import partial
import math

import jax
import jax.numpy as jnp
from jax import lax
from jax.experimental import pallas as pl
from jax.experimental.pallas import tpu as pltpu
from jax.sharding import PartitionSpec as P

HEAD = 128
BLOCK = 128
TILE = 256
GROUPS = 2
FOLD = 8
ROWS = FOLD * BLOCK
MASKED = -1e30
SCALE = 1.0 / math.sqrt(HEAD)
SCALE_LOG2E = SCALE * math.log2(math.e)

TERM_ROWS = 2 * GROUPS * HEAD + 16
DIGIT = 32

NT = (((1,), (1,)), ((), ()))
NN = (((1,), (0,)), ((), ()))


def dot(a, b, dims=NN):
    return lax.dot_general(a, b, dims, preferred_element_type=jnp.float32)


def attention_kernel(
    me_ref,
    count_ref,
    docs_ref,
    live_own,
    live_sib,
    q_own,
    q_sib,
    c_own,
    c_sib,
    *refs,
):
    chips = 8
    chunks = refs[:chips]
    o_own, o_sib, dq_own, dq_sib = refs[chips : chips + 4]
    terms = refs[chips + 4 : 2 * chips + 4]
    (
        k_nat,
        v_nat,
        s_ref,
        p_ref,
        q_ref,
        do_ref,
        qt_ref,
        dot_ref,
        m_ref,
        l_ref,
        o_ref,
        dq_ref,
        dkt_ref,
        dvt_ref,
    ) = refs[2 * chips + 4 :]

    me = me_ref[0]
    core, chip = me & 1, me >> 1
    line, side = chip >> 1, chip & 1
    lows = []
    for step in (0, 1, 3, 2):
        for other in range(2):
            lows.append(2 * ((line + step) & 3) + (side ^ other))

    for group in range(GROUPS):
        k_nat[group, 0:BLOCK, :] = jnp.zeros((BLOCK, HEAD), jnp.bfloat16)
        v_nat[group, 0:BLOCK, :] = jnp.zeros((BLOCK, HEAD), jnp.bfloat16)
    for at, chunk in enumerate(chunks):
        low = lows[at]
        for half in range(2):
            block = low if half == 0 else 15 - low
            place = pl.ds(pl.multiple_of((block + 1) * BLOCK, BLOCK), BLOCK)
            rows = slice(half * BLOCK, (half + 1) * BLOCK)
            for group in range(GROUPS):
                k_nat[group, place, :] = chunk[rows, group * HEAD : (group + 1) * HEAD]
                v_nat[group, place, :] = chunk[
                    rows, (GROUPS + group) * HEAD : (GROUPS + group + 1) * HEAD
                ]

    count = jnp.sum(count_ref[...].astype(jnp.float32), axis=1, keepdims=True)
    upper = jnp.floor(count * (1.0 / (DIGIT * DIGIT)))
    rest = count - upper * (DIGIT * DIGIT)
    middle = jnp.floor(rest * (1.0 / DIGIT))
    digit_row = lax.broadcasted_iota(jnp.int32, (16, 2 * BLOCK), 0)
    digits = jnp.where(digit_row == 0, rest - middle * DIGIT, 0.0)
    digits = jnp.where(digit_row == 1, middle, jnp.where(digit_row == 2, upper, digits))
    digits = digits.astype(jnp.bfloat16)

    def column(row):
        return jnp.broadcast_to(row.astype(jnp.float32), (BLOCK, BLOCK)).T[:, :1]

    all_docs = docs_ref[...].astype(jnp.float32)
    live_columns = column(live_own[...]), column(live_sib[...])
    bounds = []
    for half in range(2):
        block = chip if half == 0 else 15 - chip
        swapped = core if half == 0 else 1 - core
        own_docs = column(docs_ref[:, pl.ds(pl.multiple_of(block * BLOCK, BLOCK), BLOCK)])
        own_docs = jnp.where(
            swapped == 1, jnp.concatenate([own_docs[64:], own_docs[:64]], axis=0), own_docs
        )
        below = jnp.where(all_docs < own_docs, 1.0, 0.0)
        low_bound = jnp.sum(below, axis=1, keepdims=True)
        tiles = (block * BLOCK + BLOCK - jnp.min(low_bound).astype(jnp.int32) + TILE - 1) >> 8
        row = lax.broadcasted_iota(jnp.int32, (BLOCK, 1), 0)
        own_pos = block * BLOCK + ((row + 64 * swapped) & (BLOCK - 1))
        live = jnp.concatenate(
            [col[half * 64 : half * 64 + 64] for col in live_columns], axis=0
        )
        bounds.append((tiles, low_bound.astype(jnp.int32), own_pos, live))

    for group in range(GROUPS):
        dkt_ref[...] = jnp.zeros_like(dkt_ref)
        dvt_ref[...] = jnp.zeros_like(dvt_ref)
        for half in range(2):
            tiles, low_bound, own_pos, live = bounds[half]
            end = ((chip if half == 0 else 15 - chip) + 1) * BLOCK
            rows = slice(half * 64, half * 64 + 64)

            def columns(head):
                return slice((group * FOLD + head) * HEAD, (group * FOLD + head + 1) * HEAD)

            def from_columns(head):
                start = core * (GROUPS * FOLD * HEAD) + (group * FOLD + head) * HEAD
                return pl.ds(pl.multiple_of(start, HEAD), HEAD)

            for head in range(FOLD):
                q_ref[head * BLOCK : head * BLOCK + 64, :] = q_own[rows, from_columns(head)]
                q_ref[head * BLOCK + 64 : (head + 1) * BLOCK, :] = q_sib[rows, from_columns(head)]
            m_ref[...] = jnp.full_like(m_ref, MASKED)
            l_ref[...] = jnp.zeros_like(l_ref)
            o_ref[...] = jnp.zeros_like(o_ref)
            dq_ref[...] = jnp.zeros_like(dq_ref)

            def key_rows(j):
                return pl.ds(pl.multiple_of(end - TILE * (j + 1) + BLOCK, BLOCK), TILE)

            def tile_columns(j):
                return pl.ds(pl.multiple_of(j * TILE, TILE), TILE)

            def score_tile(j, _):
                first = end - TILE * (j + 1)
                key_pos = first + lax.broadcasted_iota(jnp.int32, (BLOCK, TILE), 1)
                bias = jnp.where((key_pos >= low_bound) & (key_pos <= own_pos), 0.0, MASKED)
                scores = dot(q_ref[...], k_nat[group, key_rows(j), :], NT)
                scores = (
                    scores.reshape(FOLD, BLOCK, TILE) * SCALE_LOG2E + bias[None]
                ).reshape(ROWS, TILE)
                s_ref[:, tile_columns(j)] = scores
                m_ref[...] = jnp.maximum(
                    m_ref[...], jnp.maximum(scores[:, :HEAD], scores[:, HEAD:])
                )
                return 0

            lax.fori_loop(0, tiles, score_tile, 0)
            m_ref[...] = jnp.broadcast_to(
                jnp.max(m_ref[...], axis=1, keepdims=True), (ROWS, HEAD)
            )

            def weight_tile(j, _):
                peak = m_ref[...]
                scores = s_ref[:, tile_columns(j)]
                left = jnp.exp2(scores[:, :HEAD] - peak)
                right = jnp.exp2(scores[:, HEAD:] - peak)
                l_ref[...] += left + right
                weights = jnp.concatenate([left, right], axis=1).astype(jnp.bfloat16)
                p_ref[:, tile_columns(j)] = weights
                o_ref[...] += dot(weights, v_nat[group, key_rows(j), :])
                return 0

            lax.fori_loop(0, tiles, weight_tile, 0)
            for head in range(FOLD):
                span = slice(head * BLOCK, (head + 1) * BLOCK)
                inverse = 1.0 / jnp.sum(l_ref[span, :], axis=1, keepdims=True)
                out = (o_ref[span, :] * inverse).astype(jnp.bfloat16)
                o_own[rows, columns(head)] = out[:64]
                o_sib[rows, columns(head)] = out[64:]
                cot = jnp.concatenate(
                    [c_own[rows, from_columns(head)], c_sib[rows, from_columns(head)]], axis=0
                )
                grad = (cot.astype(jnp.float32) * (live * inverse)).astype(jnp.bfloat16)
                do_ref[span, :] = grad
                m_ref[span, :] = jnp.broadcast_to(
                    jnp.sum(
                        grad.astype(jnp.float32) * out.astype(jnp.float32), axis=1, keepdims=True
                    ),
                    (BLOCK, HEAD),
                )
            qt_ref[...] = q_ref[...].T
            dot_ref[...] = do_ref[...].T

            def gradient_tile(j, _):
                delta = m_ref[...]
                pushes = dot(do_ref[...], v_nat[group, key_rows(j), :], NT)
                weights = p_ref[:, tile_columns(j)]
                wide = weights.astype(jnp.float32)
                slopes = jnp.concatenate(
                    [
                        wide[:, :HEAD] * (pushes[:, :HEAD] - delta),
                        wide[:, HEAD:] * (pushes[:, HEAD:] - delta),
                    ],
                    axis=1,
                ).astype(jnp.bfloat16)
                dq_ref[...] += dot(slopes, k_nat[group, key_rows(j), :])
                dkt_ref[:, key_rows(j)] += dot(qt_ref[...], slopes)
                dvt_ref[:, key_rows(j)] += dot(dot_ref[...], weights)
                return 0

            lax.fori_loop(0, tiles, gradient_tile, 0)
            for head in range(FOLD):
                span = slice(head * BLOCK, (head + 1) * BLOCK)
                out = (dq_ref[span, :] * SCALE).astype(jnp.bfloat16)
                dq_own[rows, columns(head)] = out[:64]
                dq_sib[rows, columns(head)] = out[64:]
        for at, term in enumerate(terms):
            low = lows[at]
            if group == 0:
                term[2 * GROUPS * HEAD :, :] = digits
            for half in range(2):
                block = low if half == 0 else 15 - low
                place = pl.ds(pl.multiple_of((block + 1) * BLOCK, BLOCK), BLOCK)
                lanes = slice(half * BLOCK, (half + 1) * BLOCK)
                term[group * HEAD : (group + 1) * HEAD, lanes] = (
                    dkt_ref[:, place] * SCALE
                ).astype(jnp.bfloat16)
                term[(GROUPS + group) * HEAD : (GROUPS + group + 1) * HEAD, lanes] = dvt_ref[
                    :, place
                ].astype(jnp.bfloat16)


def attention(me, count, docs, live_own, live_sib, q_own, q_sib, c_own, c_sib, chunks, interpret=False):
    vmem = pl.BlockSpec(memory_space=pltpu.VMEM)
    half_rows = jax.ShapeDtypeStruct((128, GROUPS * FOLD * HEAD), jnp.bfloat16)
    term = jax.ShapeDtypeStruct((TERM_ROWS, 2 * BLOCK), jnp.bfloat16)
    padded = 2048 + BLOCK
    most = 5
    return pl.pallas_call(
        attention_kernel,
        out_shape=(half_rows,) * 4 + (term,) * 8,
        in_specs=[pl.BlockSpec(memory_space=pltpu.SMEM)] + [vmem] * 16,
        out_specs=(vmem,) * 12,
        scratch_shapes=[
            pltpu.VMEM((GROUPS, padded, HEAD), jnp.bfloat16),
            pltpu.VMEM((GROUPS, padded, HEAD), jnp.bfloat16),
            pltpu.VMEM((ROWS, most * TILE), jnp.float32),
            pltpu.VMEM((ROWS, most * TILE), jnp.bfloat16),
            pltpu.VMEM((ROWS, HEAD), jnp.bfloat16),
            pltpu.VMEM((ROWS, HEAD), jnp.bfloat16),
            pltpu.VMEM((HEAD, ROWS), jnp.bfloat16),
            pltpu.VMEM((HEAD, ROWS), jnp.bfloat16),
            pltpu.VMEM((ROWS, HEAD), jnp.float32),
            pltpu.VMEM((ROWS, HEAD), jnp.float32),
            pltpu.VMEM((ROWS, HEAD), jnp.float32),
            pltpu.VMEM((ROWS, HEAD), jnp.float32),
            pltpu.VMEM((HEAD, padded), jnp.float32),
            pltpu.VMEM((HEAD, padded), jnp.float32),
        ],
        compiler_params=pltpu.CompilerParams(vmem_limit_bytes=20 * 1024 * 1024),
        cost_estimate=pl.CostEstimate(
            flops=6_000_000_000, bytes_accessed=8_000_000, transcendentals=4_000_000
        ),
        interpret=interpret,
    )(me, count, docs, live_own, live_sib, q_own, q_sib, c_own, c_sib, *chunks)


def closing_kernel(me_ref, *refs):
    terms, (kept, sent, ratio) = refs[:4], refs[4:]
    total = sum(term[...].astype(jnp.float32) for term in terms)
    width = 2 * GROUPS * HEAD
    digits = total[width : width + 8, :HEAD]
    count = digits[0:1] + DIGIT * (digits[1:2] + DIGIT * digits[2:3])
    ratio_row = 32768.0 / count
    ratio[...] = jnp.broadcast_to(ratio_row, (8, HEAD))
    rows = (total[:width] * ratio_row[:, :1]).T
    outer = jnp.concatenate([rows[:64], rows[192:]], axis=0).astype(jnp.bfloat16)
    inner = rows[64:192].astype(jnp.bfloat16)
    first = (me_ref[0] & 1) == 0
    kept[...] = jnp.where(first, outer, inner)
    sent[...] = jnp.where(first, inner, outer)


def closing(me, terms):
    vmem = pl.BlockSpec(memory_space=pltpu.VMEM)
    rows = jax.ShapeDtypeStruct((BLOCK, 2 * GROUPS * HEAD), jnp.bfloat16)
    return pl.pallas_call(
        closing_kernel,
        out_shape=(rows, rows, jax.ShapeDtypeStruct((8, HEAD), jnp.float32)),
        in_specs=[pl.BlockSpec(memory_space=pltpu.SMEM)] + [vmem] * 4,
        out_specs=(vmem,) * 3,
        compiler_params=pltpu.CompilerParams(vmem_limit_bytes=8 * 1024 * 1024),
        cost_estimate=pl.CostEstimate(flops=1_000_000, bytes_accessed=1_000_000, transcendentals=0),
    )(me, *terms)


def on_device(queries, keys, values, cotangent, live, docs):
    me = lax.axis_index("ctx")
    core = me % 2

    def move(shift):
        return [(i, (i + shift) % 16) for i in range(16)]

    def swap(bit):
        return [(i, i ^ bit) for i in range(16)]

    def to_right(a):
        return lax.ppermute(a, "ctx", move(4))

    def to_left(a):
        return lax.ppermute(a, "ctx", move(-4))

    def to_side(a):
        return lax.ppermute(a, "ctx", swap(2))

    def to_core(a):
        return lax.ppermute(a, "ctx", swap(1))

    kv_width = GROUPS * HEAD
    q_width = GROUPS * FOLD * HEAD
    keys_got, values_got = to_core(keys[0]), to_core(values[0])
    q_got, c_got = to_core(queries[0]), to_core(cotangent[0])

    def groups(a, b):
        chosen = [jnp.where(core == 0, x[:, :kv_width], x[:, kv_width:]) for x in (a, b)]
        return jnp.concatenate(chosen, axis=1)

    kv_keep, kv_got = groups(keys[0], values[0]), groups(keys_got, values_got)
    first = jnp.where(core == 0, kv_keep, kv_got)
    second = jnp.where(core == 0, kv_got, kv_keep)
    mine = jnp.concatenate([first[:64], second[:64], second[64:], first[64:]], axis=0)

    live_got = to_core(live)
    count = live + live_got
    for bit in (1, 2):
        count = count + lax.ppermute(count, "dp", swap(bit))

    from_left = to_right(mine)
    from_right = to_left(mine)
    beside = to_side(mine)
    beside, from_left, from_right, count = lax.optimization_barrier(
        (beside, from_left, from_right, count)
    )
    beside_left = to_right(beside)
    beside_right = to_left(beside)
    opposite = to_right(from_left)
    beside_opposite = to_left(beside_right)
    count, _, _ = lax.optimization_barrier((count, beside_left, beside_right))
    for bit in (4, 8):
        count = count + lax.ppermute(count, "dp", swap(bit))
    chunks = (
        mine,
        beside,
        from_right,
        beside_right,
        from_left,
        beside_left,
        opposite,
        beside_opposite,
    )

    device = me.reshape(1).astype(jnp.int32)
    results = attention(
        device,
        count,
        docs,
        live,
        live_got,
        queries[0],
        q_got,
        cotangent[0],
        c_got,
        chunks,
    )
    o_own, o_sib, dq_own, dq_sib = results[:4]
    t_mine, t_beside, t_right, t_beside_right, t_left, t_beside_left, t_opp, t_beside_opp = (
        results[4:]
    )

    def add(*terms):
        return sum(t.astype(jnp.float32) for t in terms).astype(jnp.bfloat16)

    opp_via_right = to_right(t_opp)
    opp_via_left = to_left(t_beside_opp)
    got_beside_1 = to_right(t_beside_right)
    right_sum, left_sum = add(t_right, opp_via_right), add(t_beside_left, opp_via_left)
    got_mine_2 = to_right(right_sum)
    got_beside_2 = to_left(left_sum)
    got_mine_1 = to_left(t_left)
    o_sib, dq_sib, _ = lax.optimization_barrier((o_sib, dq_sib, got_beside_1))
    beside_sum = add(t_beside, got_beside_1, got_beside_2)
    got_side = to_side(beside_sum)
    kept, sent, ratio = closing(device, (t_mine, got_mine_1, got_mine_2, got_side))
    got = to_core(sent)

    o_got, dq_got = to_core(o_sib), to_core(dq_sib)

    def join(own, got, width):
        low = jnp.where(core == 0, own, got)
        high = jnp.where(core == 0, got, own)
        return jnp.concatenate([low, high], axis=1)

    attended = join(o_own, o_got, q_width)[None]
    grad_queries = (join(dq_own, dq_got, q_width).astype(jnp.float32) * ratio[0, 0]).astype(
        jnp.bfloat16
    )[None]

    def gradient(at):
        columns = slice(at * kv_width, (at + 1) * kv_width)
        return join(kept[:, columns], got[:, columns], kv_width)[None]

    return attended, grad_queries, gradient(0), gradient(1)


def solution(mesh):
    rows = P("dp", "ctx", None)
    return jax.shard_map(
        on_device,
        mesh=mesh,
        in_specs=(rows, rows, rows, rows, P("dp", "ctx"), P("dp", None)),
        out_specs=(rows, rows, rows, rows),
        check_vma=False,
    )
```

```python
from functools import partial
import math

import jax
import jax.numpy as jnp
from jax import lax
from jax.experimental import pallas as pl
from jax.experimental.pallas import tpu as pltpu
from jax.sharding import PartitionSpec as P

HEAD = 128
BLOCK = 128
TILE = 256
GROUPS = 2
FOLD = 8
ROWS = FOLD * BLOCK
MASKED = -1e30
SCALE = 1.0 / math.sqrt(HEAD)
SCALE_LOG2E = SCALE * math.log2(math.e)

TERM_ROWS = 2 * GROUPS * HEAD + 16
DIGIT = 32

NT = (((1,), (1,)), ((), ()))
NN = (((1,), (0,)), ((), ()))


def dot(a, b, dims=NN):
    return lax.dot_general(a, b, dims, preferred_element_type=jnp.float32)


def attention_kernel(
    me_ref,
    count_ref,
    docs_ref,
    live_own,
    live_sib,
    q_own,
    q_sib,
    c_own,
    c_sib,
    *refs,
):
    chips = 8
    chunks = refs[:chips]
    o_own, dq_own, sib_out = refs[chips : chips + 3]
    terms = refs[chips + 3 : 2 * chips + 3]
    (
        k_nat,
        v_nat,
        s_ref,
        p_ref,
        q_ref,
        do_ref,
        qt_ref,
        dot_ref,
        m_ref,
        o_ref,
        dq_ref,
        dkt_ref,
        dvt_ref,
    ) = refs[2 * chips + 3 :]

    me = me_ref[0]
    core, chip = me & 1, me >> 1
    line, side = chip >> 1, chip & 1
    lows = []
    for step in (0, 1, 3, 2):
        for other in range(2):
            lows.append(2 * ((line + step) & 3) + (side ^ other))

    for group in range(GROUPS):
        k_nat[group, 0:BLOCK, :] = jnp.zeros((BLOCK, HEAD), jnp.bfloat16)
        v_nat[group, 0:BLOCK, :HEAD] = jnp.zeros((BLOCK, HEAD), jnp.bfloat16)
        v_nat[group, :, HEAD:] = jnp.ones((v_nat.shape[1], HEAD), jnp.bfloat16)
    for at, chunk in enumerate(chunks):
        low = lows[at]
        for half in range(2):
            block = low if half == 0 else 15 - low
            place = pl.ds(pl.multiple_of((block + 1) * BLOCK, BLOCK), BLOCK)
            rows = slice(half * BLOCK, (half + 1) * BLOCK)
            for group in range(GROUPS):
                k_nat[group, place, :] = chunk[rows, group * HEAD : (group + 1) * HEAD]
                v_nat[group, place, :HEAD] = chunk[
                    rows, (GROUPS + group) * HEAD : (GROUPS + group + 1) * HEAD
                ]

    count = jnp.sum(count_ref[...].astype(jnp.float32), axis=1, keepdims=True)
    upper = jnp.floor(count * (1.0 / (DIGIT * DIGIT)))
    rest = count - upper * (DIGIT * DIGIT)
    middle = jnp.floor(rest * (1.0 / DIGIT))
    digit_row = lax.broadcasted_iota(jnp.int32, (16, 2 * BLOCK), 0)
    digits = jnp.where(digit_row == 0, rest - middle * DIGIT, 0.0)
    digits = jnp.where(digit_row == 1, middle, jnp.where(digit_row == 2, upper, digits))
    digits = digits.astype(jnp.bfloat16)

    def column(row):
        return jnp.broadcast_to(row.astype(jnp.float32), (BLOCK, BLOCK)).T[:, :1]

    all_docs = docs_ref[...].astype(jnp.float32)
    live_columns = column(live_own[...]), column(live_sib[...])
    bounds = []
    for half in range(2):
        block = chip if half == 0 else 15 - chip
        swapped = core if half == 0 else 1 - core
        own_docs = column(docs_ref[:, pl.ds(pl.multiple_of(block * BLOCK, BLOCK), BLOCK)])
        own_docs = jnp.where(
            swapped == 1, jnp.concatenate([own_docs[64:], own_docs[:64]], axis=0), own_docs
        )
        below = jnp.where(all_docs < own_docs, 1.0, 0.0)
        low_bound = jnp.sum(below, axis=1, keepdims=True)
        tiles = (block * BLOCK + BLOCK - jnp.min(low_bound).astype(jnp.int32) + TILE - 1) >> 8
        row = lax.broadcasted_iota(jnp.int32, (BLOCK, 1), 0)
        own_pos = block * BLOCK + ((row + 64 * swapped) & (BLOCK - 1))
        live = jnp.concatenate(
            [col[half * 64 : half * 64 + 64] for col in live_columns], axis=0
        )
        bounds.append((tiles, low_bound.astype(jnp.int32), own_pos, live))

    for group in range(GROUPS):
        dkt_ref[...] = jnp.zeros_like(dkt_ref)
        dvt_ref[...] = jnp.zeros_like(dvt_ref)
        for half in range(2):
            tiles, low_bound, own_pos, live = bounds[half]
            end = ((chip if half == 0 else 15 - chip) + 1) * BLOCK
            rows = slice(half * 64, half * 64 + 64)
            dq_rows = slice(BLOCK + half * 64, BLOCK + half * 64 + 64)

            def columns(head):
                return slice((group * FOLD + head) * HEAD, (group * FOLD + head + 1) * HEAD)

            def from_columns(head):
                start = core * (GROUPS * FOLD * HEAD) + (group * FOLD + head) * HEAD
                return pl.ds(pl.multiple_of(start, HEAD), HEAD)

            for head in range(FOLD):
                q_ref[head * BLOCK : head * BLOCK + 64, :] = q_own[rows, from_columns(head)]
                q_ref[head * BLOCK + 64 : (head + 1) * BLOCK, :] = q_sib[rows, from_columns(head)]

            def key_rows(j):
                return pl.ds(pl.multiple_of(end - TILE * (j + 1) + BLOCK, BLOCK), TILE)

            def tile_columns(j):
                return pl.ds(pl.multiple_of(j * TILE, TILE), TILE)

            def over_tiles(body):
                body(0, True)

                @pl.loop(1, tiles)
                def _(j):
                    body(j, False)

            def score_tile(j, first_tile):
                first = end - TILE * (j + 1)
                key_pos = first + lax.broadcasted_iota(jnp.int32, (BLOCK, TILE), 1)
                bias = jnp.where((key_pos >= low_bound) & (key_pos <= own_pos), 0.0, MASKED)
                scores = dot(q_ref[...], k_nat[group, key_rows(j), :], NT)
                scores = (
                    scores.reshape(FOLD, BLOCK, TILE) * SCALE_LOG2E + bias[None]
                ).reshape(ROWS, TILE)
                s_ref[:, tile_columns(j)] = scores
                peak = jnp.maximum(scores[:, :HEAD], scores[:, HEAD:])
                m_ref[...] = peak if first_tile else jnp.maximum(m_ref[...], peak)

            over_tiles(score_tile)
            m_ref[...] = jnp.broadcast_to(
                jnp.max(m_ref[...], axis=1, keepdims=True), (ROWS, HEAD)
            )

            def weight_tile(j, first_tile):
                peak = m_ref[...]
                scores = s_ref[:, tile_columns(j)]
                left = jnp.exp2(scores[:, :HEAD] - peak)
                right = jnp.exp2(scores[:, HEAD:] - peak)
                weights = jnp.concatenate([left, right], axis=1).astype(jnp.bfloat16)
                p_ref[:, tile_columns(j)] = weights
                part = dot(weights, v_nat[group, key_rows(j), :])
                o_ref[...] = part if first_tile else o_ref[...] + part

            over_tiles(weight_tile)
            for head in range(FOLD):
                span = slice(head * BLOCK, (head + 1) * BLOCK)
                inverse = 1.0 / o_ref[span, HEAD:]
                out = (o_ref[span, :HEAD] * inverse).astype(jnp.bfloat16)
                o_own[rows, columns(head)] = out[:64]
                sib_out[rows, columns(head)] = out[64:]
                cot = jnp.concatenate(
                    [c_own[rows, from_columns(head)], c_sib[rows, from_columns(head)]], axis=0
                )
                grad = (cot.astype(jnp.float32) * (live * inverse)).astype(jnp.bfloat16)
                do_ref[span, :] = grad
                m_ref[span, :] = jnp.broadcast_to(
                    jnp.sum(
                        grad.astype(jnp.float32) * out.astype(jnp.float32), axis=1, keepdims=True
                    ),
                    (BLOCK, HEAD),
                )
            qt_ref[...] = q_ref[...].T
            dot_ref[...] = do_ref[...].T

            def gradient_tile(j, first_tile):
                delta = m_ref[...]
                pushes = dot(do_ref[...], v_nat[group, key_rows(j), :HEAD], NT)
                weights = p_ref[:, tile_columns(j)]
                wide = weights.astype(jnp.float32)
                slopes = jnp.concatenate(
                    [
                        wide[:, :HEAD] * (pushes[:, :HEAD] - delta),
                        wide[:, HEAD:] * (pushes[:, HEAD:] - delta),
                    ],
                    axis=1,
                ).astype(jnp.bfloat16)
                part = dot(slopes, k_nat[group, key_rows(j), :])
                dq_ref[...] = part if first_tile else dq_ref[...] + part
                dkt_ref[:, key_rows(j)] += dot(qt_ref[...], slopes)
                dvt_ref[:, key_rows(j)] += dot(dot_ref[...], weights)

            over_tiles(gradient_tile)
            for head in range(FOLD):
                span = slice(head * BLOCK, (head + 1) * BLOCK)
                out = (dq_ref[span, :] * SCALE).astype(jnp.bfloat16)
                dq_own[rows, columns(head)] = out[:64]
                sib_out[dq_rows, columns(head)] = out[64:]
        for at, term in enumerate(terms):
            low = lows[at]
            if group == 0:
                term[2 * GROUPS * HEAD :, :] = digits
            for half in range(2):
                block = low if half == 0 else 15 - low
                place = pl.ds(pl.multiple_of((block + 1) * BLOCK, BLOCK), BLOCK)
                lanes = slice(half * BLOCK, (half + 1) * BLOCK)
                term[group * HEAD : (group + 1) * HEAD, lanes] = (
                    dkt_ref[:, place] * SCALE
                ).astype(jnp.bfloat16)
                term[(GROUPS + group) * HEAD : (GROUPS + group + 1) * HEAD, lanes] = dvt_ref[
                    :, place
                ].astype(jnp.bfloat16)


def attention(me, count, docs, live_own, live_sib, q_own, q_sib, c_own, c_sib, chunks, interpret=False):
    vmem = pl.BlockSpec(memory_space=pltpu.VMEM)
    half_rows = jax.ShapeDtypeStruct((128, GROUPS * FOLD * HEAD), jnp.bfloat16)
    both_rows = jax.ShapeDtypeStruct((256, GROUPS * FOLD * HEAD), jnp.bfloat16)
    term = jax.ShapeDtypeStruct((TERM_ROWS, 2 * BLOCK), jnp.bfloat16)
    padded = 2048 + BLOCK
    most = 5
    return pl.pallas_call(
        attention_kernel,
        out_shape=(half_rows, half_rows, both_rows) + (term,) * 8,
        in_specs=[pl.BlockSpec(memory_space=pltpu.SMEM)] + [vmem] * 16,
        out_specs=(vmem,) * 11,
        scratch_shapes=[
            pltpu.VMEM((GROUPS, padded, HEAD), jnp.bfloat16),
            pltpu.VMEM((GROUPS, padded, 2 * HEAD), jnp.bfloat16),
            pltpu.VMEM((ROWS, most * TILE), jnp.float32),
            pltpu.VMEM((ROWS, most * TILE), jnp.bfloat16),
            pltpu.VMEM((ROWS, HEAD), jnp.bfloat16),
            pltpu.VMEM((ROWS, HEAD), jnp.bfloat16),
            pltpu.VMEM((HEAD, ROWS), jnp.bfloat16),
            pltpu.VMEM((HEAD, ROWS), jnp.bfloat16),
            pltpu.VMEM((ROWS, HEAD), jnp.float32),
            pltpu.VMEM((ROWS, 2 * HEAD), jnp.float32),
            pltpu.VMEM((ROWS, HEAD), jnp.float32),
            pltpu.VMEM((HEAD, padded), jnp.float32),
            pltpu.VMEM((HEAD, padded), jnp.float32),
        ],
        compiler_params=pltpu.CompilerParams(vmem_limit_bytes=28 * 1024 * 1024),
        cost_estimate=pl.CostEstimate(
            flops=6_000_000_000, bytes_accessed=8_000_000, transcendentals=4_000_000
        ),
        interpret=interpret,
    )(me, count, docs, live_own, live_sib, q_own, q_sib, c_own, c_sib, *chunks)


def closing_kernel(me_ref, *refs):
    terms, (kept, sent, ratio) = refs[:4], refs[4:]
    total = sum(term[...].astype(jnp.float32) for term in terms)
    width = 2 * GROUPS * HEAD
    digits = total[width : width + 8, :HEAD]
    count = digits[0:1] + DIGIT * (digits[1:2] + DIGIT * digits[2:3])
    ratio_row = 32768.0 / count
    ratio[...] = jnp.broadcast_to(ratio_row, (8, HEAD))
    rows = (total[:width] * ratio_row[:, :1]).T
    outer = jnp.concatenate([rows[:64], rows[192:]], axis=0).astype(jnp.bfloat16)
    inner = rows[64:192].astype(jnp.bfloat16)
    first = (me_ref[0] & 1) == 0
    kept[...] = jnp.where(first, outer, inner)
    sent[...] = jnp.where(first, inner, outer)


def closing(me, terms):
    vmem = pl.BlockSpec(memory_space=pltpu.VMEM)
    rows = jax.ShapeDtypeStruct((BLOCK, 2 * GROUPS * HEAD), jnp.bfloat16)
    return pl.pallas_call(
        closing_kernel,
        out_shape=(rows, rows, jax.ShapeDtypeStruct((8, HEAD), jnp.float32)),
        in_specs=[pl.BlockSpec(memory_space=pltpu.SMEM)] + [vmem] * 4,
        out_specs=(vmem,) * 3,
        compiler_params=pltpu.CompilerParams(vmem_limit_bytes=8 * 1024 * 1024),
        cost_estimate=pl.CostEstimate(flops=1_000_000, bytes_accessed=1_000_000, transcendentals=0),
    )(me, *terms)


def scale_kernel(me_ref, ratio, own, got, out):
    at = pl.program_id(0)
    mine = (at >> 1) == (me_ref[0] & 1)
    columns = pl.ds(pl.multiple_of((at & 1) * 1024, 1024), 1024)
    factor = ratio[0:1, 0:1]

    @pl.when(mine)
    def _():
        out[...] = (own[:, columns].astype(jnp.float32) * factor).astype(jnp.bfloat16)

    @pl.when(jnp.logical_not(mine))
    def _():
        out[...] = (got[BLOCK:, columns].astype(jnp.float32) * factor).astype(jnp.bfloat16)


def scaled(me, ratio, own, got):
    vmem = pl.BlockSpec(memory_space=pltpu.VMEM)
    return pl.pallas_call(
        scale_kernel,
        grid=(4,),
        out_shape=jax.ShapeDtypeStruct((BLOCK, 4096), jnp.bfloat16),
        in_specs=[pl.BlockSpec(memory_space=pltpu.SMEM)] + [vmem] * 3,
        out_specs=pl.BlockSpec((BLOCK, 1024), lambda i: (0, i)),
        compiler_params=pltpu.CompilerParams(vmem_limit_bytes=8 * 1024 * 1024),
        cost_estimate=pl.CostEstimate(flops=1_000_000, bytes_accessed=2_000_000, transcendentals=0),
    )(me, ratio, own, got)


def join_kernel(me_ref, kept, got, keys, values):
    first = (me_ref[0] & 1) == 0
    width = GROUPS * HEAD
    for at, out in enumerate((keys, values)):
        columns = slice(at * width, (at + 1) * width)
        own, other = kept[:, columns], got[:, columns]
        out[:, :width] = jnp.where(first, own, other)
        out[:, width:] = jnp.where(first, other, own)


def joined(me, kept, got):
    vmem = pl.BlockSpec(memory_space=pltpu.VMEM)
    whole = pl.BlockSpec((BLOCK, 2 * GROUPS * HEAD), lambda i: (0, 0))
    rows = jax.ShapeDtypeStruct((BLOCK, 2 * GROUPS * HEAD), jnp.bfloat16)
    return pl.pallas_call(
        join_kernel,
        grid=(1,),
        out_shape=(rows, rows),
        in_specs=[pl.BlockSpec(memory_space=pltpu.SMEM)] + [vmem] * 2,
        out_specs=(whole, whole),
        compiler_params=pltpu.CompilerParams(vmem_limit_bytes=4 * 1024 * 1024),
        cost_estimate=pl.CostEstimate(flops=100_000, bytes_accessed=500_000, transcendentals=0),
    )(me, kept, got)


def on_device(queries, keys, values, cotangent, live, docs):
    me = lax.axis_index("ctx")
    core = me % 2

    def move(shift):
        return [(i, (i + shift) % 16) for i in range(16)]

    def swap(bit):
        return [(i, i ^ bit) for i in range(16)]

    def to_right(a):
        return lax.ppermute(a, "ctx", move(4))

    def to_left(a):
        return lax.ppermute(a, "ctx", move(-4))

    def to_side(a):
        return lax.ppermute(a, "ctx", swap(2))

    def to_core(a):
        return lax.ppermute(a, "ctx", swap(1))

    kv_width = GROUPS * HEAD
    q_width = GROUPS * FOLD * HEAD
    keys_got, values_got = to_core(keys[0]), to_core(values[0])
    q_got, c_got = to_core(queries[0]), to_core(cotangent[0])

    def groups(a, b):
        chosen = [jnp.where(core == 0, x[:, :kv_width], x[:, kv_width:]) for x in (a, b)]
        return jnp.concatenate(chosen, axis=1)

    kv_keep, kv_got = groups(keys[0], values[0]), groups(keys_got, values_got)
    first = jnp.where(core == 0, kv_keep, kv_got)
    second = jnp.where(core == 0, kv_got, kv_keep)
    mine = jnp.concatenate([first[:64], second[:64], second[64:], first[64:]], axis=0)

    live_got = to_core(live)
    count = live + live_got
    for bit in (1, 2):
        count = count + lax.ppermute(count, "dp", swap(bit))
    count, _ = lax.optimization_barrier((count, mine))
    count = count + lax.ppermute(count, "dp", swap(4))

    from_left = to_right(mine)
    from_right = to_left(mine)
    beside = to_side(mine)
    beside, from_left, from_right, count = lax.optimization_barrier(
        (beside, from_left, from_right, count)
    )
    beside_left = to_right(beside)
    beside_right = to_left(beside)
    opposite = to_right(from_left)
    beside_opposite = to_left(beside_right)
    count, _, _ = lax.optimization_barrier((count, beside_left, beside_right))
    count = count + lax.ppermute(count, "dp", swap(8))
    chunks = (
        mine,
        beside,
        from_right,
        beside_right,
        from_left,
        beside_left,
        opposite,
        beside_opposite,
    )

    device = me.reshape(1).astype(jnp.int32)
    results = attention(
        device,
        count,
        docs,
        live,
        live_got,
        queries[0],
        q_got,
        cotangent[0],
        c_got,
        chunks,
    )
    o_own, dq_own, sib_out = results[:3]
    sib_got = to_core(sib_out)
    t_mine, t_beside, t_right, t_beside_right, t_left, t_beside_left, t_opp, t_beside_opp = (
        results[3:]
    )

    def add(*terms):
        return sum(t.astype(jnp.float32) for t in terms).astype(jnp.bfloat16)

    opp_via_right = to_right(t_opp)
    opp_via_left = to_left(t_beside_opp)
    got_beside_1 = to_right(t_beside_right)
    right_sum, left_sum = add(t_right, opp_via_right), add(t_beside_left, opp_via_left)
    got_mine_2 = to_right(right_sum)
    got_beside_2 = to_left(left_sum)
    got_mine_1 = to_left(t_left)
    beside_sum = add(t_beside, got_beside_1, got_beside_2)
    got_side = to_side(beside_sum)
    def join(own, got, width):
        low = jnp.where(core == 0, own, got)
        high = jnp.where(core == 0, got, own)
        return jnp.concatenate([low, high], axis=1)

    attended = join(o_own, sib_got[:BLOCK], q_width)[None]
    t_mine, attended = lax.optimization_barrier((t_mine, attended))
    kept, sent, ratio = closing(device, (t_mine, got_mine_1, got_mine_2, got_side))
    got = to_core(sent)

    grad_queries = scaled(device, ratio, dq_own, sib_got)[None]
    got, grad_queries = lax.optimization_barrier((got, grad_queries))
    key_gradient, value_gradient = joined(device, kept, got)
    return attended, grad_queries, key_gradient[None], value_gradient[None]


def solution(mesh):
    rows = P("dp", "ctx", None)
    return jax.shard_map(
        on_device,
        mesh=mesh,
        in_specs=(rows, rows, rows, rows, P("dp", "ctx"), P("dp", None)),
        out_specs=(rows, rows, rows, rows),
        check_vma=False,
    )
```

```python
from functools import partial
import math

import jax
import jax.numpy as jnp
from jax import lax
from jax.experimental import pallas as pl
from jax.experimental.pallas import tpu as pltpu
from jax.sharding import PartitionSpec as P

HEAD = 128
BLOCK = 128
TILE = 256
GROUPS = 2
FOLD = 8
ROWS = FOLD * BLOCK
MASKED = -1e30
SCALE = 1.0 / math.sqrt(HEAD)
SCALE_LOG2E = SCALE * math.log2(math.e)

TERM_ROWS = 2 * GROUPS * HEAD + 16
DIGIT = 32

NT = (((1,), (1,)), ((), ()))
NN = (((1,), (0,)), ((), ()))


def dot(a, b, dims=NN):
    return lax.dot_general(a, b, dims, preferred_element_type=jnp.float32)


def attention_kernel(
    me_ref,
    count_ref,
    docs_ref,
    live_own,
    live_sib,
    q_own,
    q_sib,
    c_own,
    c_sib,
    *refs,
):
    chips = 8
    chunks = refs[:chips]
    o_own, dq_own, sib_out = refs[chips : chips + 3]
    terms = refs[chips + 3 : 2 * chips + 3]
    (
        k_nat,
        v_nat,
        s_ref,
        p_ref,
        q_ref,
        do_ref,
        qt_ref,
        dot_ref,
        m_ref,
        o_ref,
        dq_ref,
        dkt_ref,
        dvt_ref,
    ) = refs[2 * chips + 3 :]

    me = me_ref[0]
    core, chip = me & 1, me >> 1
    line, side = chip >> 1, chip & 1
    lows = []
    for step in (0, 1, 3, 2):
        for other in range(2):
            lows.append(2 * ((line + step) & 3) + (side ^ other))

    for group in range(GROUPS):
        k_nat[group, 0:BLOCK, :] = jnp.zeros((BLOCK, HEAD), jnp.bfloat16)
        v_nat[group, 0:BLOCK, :HEAD] = jnp.zeros((BLOCK, HEAD), jnp.bfloat16)
        v_nat[group, :, HEAD:] = jnp.ones((v_nat.shape[1], HEAD), jnp.bfloat16)
    for at, chunk in enumerate(chunks):
        low = lows[at]
        for half in range(2):
            block = low if half == 0 else 15 - low
            place = pl.ds(pl.multiple_of((block + 1) * BLOCK, BLOCK), BLOCK)
            rows = slice(half * BLOCK, (half + 1) * BLOCK)
            for group in range(GROUPS):
                k_nat[group, place, :] = chunk[rows, group * HEAD : (group + 1) * HEAD]
                v_nat[group, place, :HEAD] = chunk[
                    rows, (GROUPS + group) * HEAD : (GROUPS + group + 1) * HEAD
                ]

    count = jnp.sum(count_ref[...].astype(jnp.float32), axis=1, keepdims=True)
    upper = jnp.floor(count * (1.0 / (DIGIT * DIGIT)))
    rest = count - upper * (DIGIT * DIGIT)
    middle = jnp.floor(rest * (1.0 / DIGIT))
    digit_row = lax.broadcasted_iota(jnp.int32, (16, 2 * BLOCK), 0)
    digits = jnp.where(digit_row == 0, rest - middle * DIGIT, 0.0)
    digits = jnp.where(digit_row == 1, middle, jnp.where(digit_row == 2, upper, digits))
    digits = digits.astype(jnp.bfloat16)

    def column(row):
        return jnp.broadcast_to(row.astype(jnp.float32), (BLOCK, BLOCK)).T[:, :1]

    all_docs = docs_ref[...].astype(jnp.float32)
    live_columns = column(live_own[...]), column(live_sib[...])
    bounds = []
    for half in range(2):
        block = chip if half == 0 else 15 - chip
        swapped = core if half == 0 else 1 - core
        own_docs = column(docs_ref[:, pl.ds(pl.multiple_of(block * BLOCK, BLOCK), BLOCK)])
        own_docs = jnp.where(
            swapped == 1, jnp.concatenate([own_docs[64:], own_docs[:64]], axis=0), own_docs
        )
        below = jnp.where(all_docs < own_docs, 1.0, 0.0)
        low_bound = jnp.sum(below, axis=1, keepdims=True)
        tiles = (block * BLOCK + BLOCK - jnp.min(low_bound).astype(jnp.int32) + TILE - 1) >> 8
        row = lax.broadcasted_iota(jnp.int32, (BLOCK, 1), 0)
        own_pos = block * BLOCK + ((row + 64 * swapped) & (BLOCK - 1))
        live = jnp.concatenate(
            [col[half * 64 : half * 64 + 64] for col in live_columns], axis=0
        )
        bounds.append((tiles, low_bound.astype(jnp.int32), own_pos, live))

    for group in range(GROUPS):
        dkt_ref[...] = jnp.zeros_like(dkt_ref)
        dvt_ref[...] = jnp.zeros_like(dvt_ref)
        for half in range(2):
            tiles, low_bound, own_pos, live = bounds[half]
            end = ((chip if half == 0 else 15 - chip) + 1) * BLOCK
            rows = slice(half * 64, half * 64 + 64)
            dq_rows = slice(BLOCK + half * 64, BLOCK + half * 64 + 64)

            def columns(head):
                return slice((group * FOLD + head) * HEAD, (group * FOLD + head + 1) * HEAD)

            def from_columns(head):
                start = core * (GROUPS * FOLD * HEAD) + (group * FOLD + head) * HEAD
                return pl.ds(pl.multiple_of(start, HEAD), HEAD)

            for head in range(FOLD):
                q_ref[head * BLOCK : head * BLOCK + 64, :] = q_own[rows, from_columns(head)]
                q_ref[head * BLOCK + 64 : (head + 1) * BLOCK, :] = q_sib[rows, from_columns(head)]

            def key_rows(j):
                return pl.ds(pl.multiple_of(end - TILE * (j + 1) + BLOCK, BLOCK), TILE)

            def tile_columns(j):
                return pl.ds(pl.multiple_of(j * TILE, TILE), TILE)

            def over_tiles(body):
                body(0, True)

                @pl.loop(1, tiles)
                def _(j):
                    body(j, False)

            def score_tile(j, first_tile):
                first = end - TILE * (j + 1)
                key_pos = first + lax.broadcasted_iota(jnp.int32, (BLOCK, TILE), 1)
                bias = jnp.where((key_pos >= low_bound) & (key_pos <= own_pos), 0.0, MASKED)
                scores = dot(q_ref[...], k_nat[group, key_rows(j), :], NT)
                scores = (
                    scores.reshape(FOLD, BLOCK, TILE) * SCALE_LOG2E + bias[None]
                ).reshape(ROWS, TILE)
                s_ref[:, tile_columns(j)] = scores
                peak = jnp.maximum(scores[:, :HEAD], scores[:, HEAD:])
                m_ref[...] = peak if first_tile else jnp.maximum(m_ref[...], peak)

            over_tiles(score_tile)
            m_ref[...] = jnp.broadcast_to(
                jnp.max(m_ref[...], axis=1, keepdims=True), (ROWS, HEAD)
            )

            def weight_tile(j, first_tile):
                peak = m_ref[...]
                scores = s_ref[:, tile_columns(j)]
                left = jnp.exp2(scores[:, :HEAD] - peak)
                right = jnp.exp2(scores[:, HEAD:] - peak)
                weights = jnp.concatenate([left, right], axis=1).astype(jnp.bfloat16)
                p_ref[:, tile_columns(j)] = weights
                part = dot(weights, v_nat[group, key_rows(j), :])
                o_ref[...] = part if first_tile else o_ref[...] + part

            over_tiles(weight_tile)
            for head in range(FOLD):
                span = slice(head * BLOCK, (head + 1) * BLOCK)
                inverse = 1.0 / o_ref[span, HEAD:]
                out = (o_ref[span, :HEAD] * inverse).astype(jnp.bfloat16)
                o_own[rows, columns(head)] = out[:64]
                sib_out[rows, columns(head)] = out[64:]
                cot = jnp.concatenate(
                    [c_own[rows, from_columns(head)], c_sib[rows, from_columns(head)]], axis=0
                )
                grad = (cot.astype(jnp.float32) * (live * inverse)).astype(jnp.bfloat16)
                do_ref[span, :] = grad
                m_ref[span, :] = jnp.broadcast_to(
                    jnp.sum(
                        grad.astype(jnp.float32) * out.astype(jnp.float32), axis=1, keepdims=True
                    ),
                    (BLOCK, HEAD),
                )
            qt_ref[...] = q_ref[...].T
            dot_ref[...] = do_ref[...].T

            def gradient_tile(j, first_tile):
                delta = m_ref[...]
                pushes = dot(do_ref[...], v_nat[group, key_rows(j), :HEAD], NT)
                weights = p_ref[:, tile_columns(j)]
                wide = weights.astype(jnp.float32)
                slopes = jnp.concatenate(
                    [
                        wide[:, :HEAD] * (pushes[:, :HEAD] - delta),
                        wide[:, HEAD:] * (pushes[:, HEAD:] - delta),
                    ],
                    axis=1,
                ).astype(jnp.bfloat16)
                part = dot(slopes, k_nat[group, key_rows(j), :])
                dq_ref[...] = part if first_tile else dq_ref[...] + part
                dkt_ref[:, key_rows(j)] += dot(qt_ref[...], slopes)
                dvt_ref[:, key_rows(j)] += dot(dot_ref[...], weights)

            over_tiles(gradient_tile)
            for head in range(FOLD):
                span = slice(head * BLOCK, (head + 1) * BLOCK)
                out = (dq_ref[span, :] * SCALE).astype(jnp.bfloat16)
                dq_own[rows, columns(head)] = out[:64]
                sib_out[dq_rows, columns(head)] = out[64:]
        for at, term in enumerate(terms):
            low = lows[at]
            if group == 0:
                term[2 * GROUPS * HEAD :, :] = digits
            for half in range(2):
                block = low if half == 0 else 15 - low
                place = pl.ds(pl.multiple_of((block + 1) * BLOCK, BLOCK), BLOCK)
                lanes = slice(half * BLOCK, (half + 1) * BLOCK)
                term[group * HEAD : (group + 1) * HEAD, lanes] = (
                    dkt_ref[:, place] * SCALE
                ).astype(jnp.bfloat16)
                term[(GROUPS + group) * HEAD : (GROUPS + group + 1) * HEAD, lanes] = dvt_ref[
                    :, place
                ].astype(jnp.bfloat16)


def attention(me, count, docs, live_own, live_sib, q_own, q_sib, c_own, c_sib, chunks, interpret=False):
    vmem = pl.BlockSpec(memory_space=pltpu.VMEM)
    half_rows = jax.ShapeDtypeStruct((128, GROUPS * FOLD * HEAD), jnp.bfloat16)
    both_rows = jax.ShapeDtypeStruct((256, GROUPS * FOLD * HEAD), jnp.bfloat16)
    term = jax.ShapeDtypeStruct((TERM_ROWS, 2 * BLOCK), jnp.bfloat16)
    padded = 2048 + BLOCK
    most = 5
    return pl.pallas_call(
        attention_kernel,
        out_shape=(half_rows, half_rows, both_rows) + (term,) * 8,
        in_specs=[pl.BlockSpec(memory_space=pltpu.SMEM)] + [vmem] * 16,
        out_specs=(vmem,) * 11,
        scratch_shapes=[
            pltpu.VMEM((GROUPS, padded, HEAD), jnp.bfloat16),
            pltpu.VMEM((GROUPS, padded, 2 * HEAD), jnp.bfloat16),
            pltpu.VMEM((ROWS, most * TILE), jnp.float32),
            pltpu.VMEM((ROWS, most * TILE), jnp.bfloat16),
            pltpu.VMEM((ROWS, HEAD), jnp.bfloat16),
            pltpu.VMEM((ROWS, HEAD), jnp.bfloat16),
            pltpu.VMEM((HEAD, ROWS), jnp.bfloat16),
            pltpu.VMEM((HEAD, ROWS), jnp.bfloat16),
            pltpu.VMEM((ROWS, HEAD), jnp.float32),
            pltpu.VMEM((ROWS, 2 * HEAD), jnp.float32),
            pltpu.VMEM((ROWS, HEAD), jnp.float32),
            pltpu.VMEM((HEAD, padded), jnp.float32),
            pltpu.VMEM((HEAD, padded), jnp.float32),
        ],
        compiler_params=pltpu.CompilerParams(vmem_limit_bytes=28 * 1024 * 1024),
        cost_estimate=pl.CostEstimate(
            flops=6_000_000_000, bytes_accessed=8_000_000, transcendentals=4_000_000
        ),
        interpret=interpret,
    )(me, count, docs, live_own, live_sib, q_own, q_sib, c_own, c_sib, *chunks)


def closing_kernel(me_ref, *refs):
    terms, (kept, sent, ratio) = refs[:4], refs[4:]
    total = sum(term[...].astype(jnp.float32) for term in terms)
    width = 2 * GROUPS * HEAD
    digits = total[width : width + 8, :HEAD]
    count = digits[0:1] + DIGIT * (digits[1:2] + DIGIT * digits[2:3])
    ratio_row = 32768.0 / count
    ratio[...] = jnp.broadcast_to(ratio_row, (8, HEAD))
    rows = (total[:width] * ratio_row[:, :1]).T
    outer = jnp.concatenate([rows[:64], rows[192:]], axis=0).astype(jnp.bfloat16)
    inner = rows[64:192].astype(jnp.bfloat16)
    first = (me_ref[0] & 1) == 0
    kept[...] = jnp.where(first, outer, inner)
    sent[...] = jnp.where(first, inner, outer)


def closing(me, terms):
    vmem = pl.BlockSpec(memory_space=pltpu.VMEM)
    rows = jax.ShapeDtypeStruct((BLOCK, 2 * GROUPS * HEAD), jnp.bfloat16)
    return pl.pallas_call(
        closing_kernel,
        out_shape=(rows, rows, jax.ShapeDtypeStruct((8, HEAD), jnp.float32)),
        in_specs=[pl.BlockSpec(memory_space=pltpu.SMEM)] + [vmem] * 4,
        out_specs=(vmem,) * 3,
        compiler_params=pltpu.CompilerParams(vmem_limit_bytes=8 * 1024 * 1024),
        cost_estimate=pl.CostEstimate(flops=1_000_000, bytes_accessed=1_000_000, transcendentals=0),
    )(me, *terms)


def scale_kernel(me_ref, ratio, own, got, out):
    at = pl.program_id(0)
    mine = (at >> 1) == (me_ref[0] & 1)
    columns = pl.ds(pl.multiple_of((at & 1) * 1024, 1024), 1024)
    factor = ratio[0:1, 0:1]

    @pl.when(mine)
    def _():
        out[...] = (own[:, columns].astype(jnp.float32) * factor).astype(jnp.bfloat16)

    @pl.when(jnp.logical_not(mine))
    def _():
        out[...] = (got[BLOCK:, columns].astype(jnp.float32) * factor).astype(jnp.bfloat16)


def scaled(me, ratio, own, got):
    vmem = pl.BlockSpec(memory_space=pltpu.VMEM)
    return pl.pallas_call(
        scale_kernel,
        grid=(4,),
        out_shape=jax.ShapeDtypeStruct((BLOCK, 4096), jnp.bfloat16),
        in_specs=[pl.BlockSpec(memory_space=pltpu.SMEM)] + [vmem] * 3,
        out_specs=pl.BlockSpec((BLOCK, 1024), lambda i: (0, i)),
        compiler_params=pltpu.CompilerParams(vmem_limit_bytes=8 * 1024 * 1024),
        cost_estimate=pl.CostEstimate(flops=1_000_000, bytes_accessed=2_000_000, transcendentals=0),
    )(me, ratio, own, got)


def join_kernel(me_ref, kept, got, keys, values):
    first = (me_ref[0] & 1) == 0
    width = GROUPS * HEAD
    for at, out in enumerate((keys, values)):
        columns = slice(at * width, (at + 1) * width)
        own, other = kept[:, columns], got[:, columns]
        out[:, :width] = jnp.where(first, own, other)
        out[:, width:] = jnp.where(first, other, own)


def joined(me, kept, got):
    vmem = pl.BlockSpec(memory_space=pltpu.VMEM)
    whole = pl.BlockSpec((BLOCK, 2 * GROUPS * HEAD), lambda i: (0, 0))
    rows = jax.ShapeDtypeStruct((BLOCK, 2 * GROUPS * HEAD), jnp.bfloat16)
    return pl.pallas_call(
        join_kernel,
        grid=(1,),
        out_shape=(rows, rows),
        in_specs=[pl.BlockSpec(memory_space=pltpu.SMEM)] + [vmem] * 2,
        out_specs=(whole, whole),
        compiler_params=pltpu.CompilerParams(vmem_limit_bytes=4 * 1024 * 1024),
        cost_estimate=pl.CostEstimate(flops=100_000, bytes_accessed=500_000, transcendentals=0),
    )(me, kept, got)


def on_device(queries, keys, values, cotangent, live, docs):
    me = lax.axis_index("ctx")
    core = me % 2

    def move(shift):
        return [(i, (i + shift) % 16) for i in range(16)]

    def swap(bit):
        return [(i, i ^ bit) for i in range(16)]

    def to_right(a):
        return lax.ppermute(a, "ctx", move(4))

    def to_left(a):
        return lax.ppermute(a, "ctx", move(-4))

    def to_side(a):
        return lax.ppermute(a, "ctx", swap(2))

    def to_core(a):
        return lax.ppermute(a, "ctx", swap(1))

    kv_width = GROUPS * HEAD
    q_width = GROUPS * FOLD * HEAD
    keys_got, values_got = to_core(keys[0]), to_core(values[0])
    q_got, c_got = to_core(queries[0]), to_core(cotangent[0])

    def groups(a, b):
        chosen = [jnp.where(core == 0, x[:, :kv_width], x[:, kv_width:]) for x in (a, b)]
        return jnp.concatenate(chosen, axis=1)

    kv_keep, kv_got = groups(keys[0], values[0]), groups(keys_got, values_got)
    first = jnp.where(core == 0, kv_keep, kv_got)
    second = jnp.where(core == 0, kv_got, kv_keep)
    mine = jnp.concatenate([first[:64], second[:64], second[64:], first[64:]], axis=0)

    live_got = to_core(live)
    count = live + live_got
    for bit in (1, 2):
        count = count + lax.ppermute(count, "dp", swap(bit))
    count, _ = lax.optimization_barrier((count, mine))
    count = count + lax.ppermute(count, "dp", swap(8))

    from_left = to_right(mine)
    from_right = to_left(mine)
    beside = to_side(mine)
    beside, from_left, from_right, count = lax.optimization_barrier(
        (beside, from_left, from_right, count)
    )
    beside_left = to_right(beside)
    beside_right = to_left(beside)
    opposite = to_right(from_left)
    beside_opposite = to_left(beside_right)
    count, _, _ = lax.optimization_barrier((count, beside_left, beside_right))
    count = count + lax.ppermute(count, "dp", swap(4))
    chunks = (
        mine,
        beside,
        from_right,
        beside_right,
        from_left,
        beside_left,
        opposite,
        beside_opposite,
    )

    device = me.reshape(1).astype(jnp.int32)
    results = attention(
        device,
        count,
        docs,
        live,
        live_got,
        queries[0],
        q_got,
        cotangent[0],
        c_got,
        chunks,
    )
    o_own, dq_own, sib_out = results[:3]
    sib_got = to_core(sib_out)
    t_mine, t_beside, t_right, t_beside_right, t_left, t_beside_left, t_opp, t_beside_opp = (
        results[3:]
    )

    def add(*terms):
        return sum(t.astype(jnp.float32) for t in terms).astype(jnp.bfloat16)

    opp_via_right = to_right(t_opp)
    opp_via_left = to_left(t_beside_opp)
    got_beside_1 = to_right(t_beside_right)
    right_sum, left_sum = add(t_right, opp_via_right), add(t_beside_left, opp_via_left)
    got_mine_2 = to_right(right_sum)
    got_beside_2 = to_left(left_sum)
    got_mine_1 = to_left(t_left)
    beside_sum = add(t_beside, got_beside_1, got_beside_2)
    got_side = to_side(beside_sum)
    def join(own, got, width):
        low = jnp.where(core == 0, own, got)
        high = jnp.where(core == 0, got, own)
        return jnp.concatenate([low, high], axis=1)

    attended = join(o_own, sib_got[:BLOCK], q_width)[None]
    t_mine, attended = lax.optimization_barrier((t_mine, attended))
    kept, sent, ratio = closing(device, (t_mine, got_mine_1, got_mine_2, got_side))
    got = to_core(sent)

    grad_queries = scaled(device, ratio, dq_own, sib_got)[None]
    got, grad_queries = lax.optimization_barrier((got, grad_queries))
    key_gradient, value_gradient = joined(device, kept, got)
    return attended, grad_queries, key_gradient[None], value_gradient[None]


def solution(mesh):
    rows = P("dp", "ctx", None)
    return jax.shard_map(
        on_device,
        mesh=mesh,
        in_specs=(rows, rows, rows, rows, P("dp", "ctx"), P("dp", None)),
        out_specs=(rows, rows, rows, rows),
        check_vma=False,
    )
```

```python
from functools import partial
import math

import jax
import jax.numpy as jnp
from jax import lax
from jax.experimental import pallas as pl
from jax.experimental.pallas import tpu as pltpu
from jax.sharding import PartitionSpec as P

HEAD = 128
BLOCK = 128
TILE = 256
GROUPS = 2
FOLD = 8
ROWS = FOLD * BLOCK
MASKED = -1e30
SCALE = 1.0 / math.sqrt(HEAD)
SCALE_LOG2E = SCALE * math.log2(math.e)

TERM_ROWS = 2 * GROUPS * HEAD + 16
DIGIT = 32

NT = (((1,), (1,)), ((), ()))
NN = (((1,), (0,)), ((), ()))


def dot(a, b, dims=NN):
    return lax.dot_general(a, b, dims, preferred_element_type=jnp.float32)


def attention_kernel(
    me_ref,
    count_ref,
    docs_ref,
    live_own,
    live_sib,
    q_own,
    q_sib,
    c_own,
    c_sib,
    *refs,
):
    chips = 8
    chunks = refs[:chips]
    o_own, dq_own, sib_out = refs[chips : chips + 3]
    terms = refs[chips + 3 : 2 * chips + 3]
    (
        k_nat,
        v_nat,
        s_ref,
        p_ref,
        q_ref,
        do_ref,
        qt_ref,
        dot_ref,
        m_ref,
        o_ref,
        dq_ref,
        dkt_ref,
        dvt_ref,
    ) = refs[2 * chips + 3 :]

    me = me_ref[0]
    core, chip = me & 1, me >> 1
    line, side = chip >> 1, chip & 1
    lows = []
    for step in (0, 1, 3, 2):
        for other in range(2):
            lows.append(2 * ((line + step) & 3) + (side ^ other))

    for group in range(GROUPS):
        k_nat[group, 0:BLOCK, :] = jnp.zeros((BLOCK, HEAD), jnp.bfloat16)
        v_nat[group, 0:BLOCK, :HEAD] = jnp.zeros((BLOCK, HEAD), jnp.bfloat16)
        v_nat[group, :, HEAD:] = jnp.ones((v_nat.shape[1], HEAD), jnp.bfloat16)
    for at, chunk in enumerate(chunks):
        low = lows[at]
        for half in range(2):
            block = low if half == 0 else 15 - low
            place = pl.ds(pl.multiple_of((block + 1) * BLOCK, BLOCK), BLOCK)
            rows = slice(half * BLOCK, (half + 1) * BLOCK)
            for group in range(GROUPS):
                k_nat[group, place, :] = chunk[rows, group * HEAD : (group + 1) * HEAD]
                v_nat[group, place, :HEAD] = chunk[
                    rows, (GROUPS + group) * HEAD : (GROUPS + group + 1) * HEAD
                ]

    count = jnp.sum(count_ref[...].astype(jnp.float32), axis=1, keepdims=True)
    upper = jnp.floor(count * (1.0 / (DIGIT * DIGIT)))
    rest = count - upper * (DIGIT * DIGIT)
    middle = jnp.floor(rest * (1.0 / DIGIT))
    digit_row = lax.broadcasted_iota(jnp.int32, (16, 2 * BLOCK), 0)
    digits = jnp.where(digit_row == 0, rest - middle * DIGIT, 0.0)
    digits = jnp.where(digit_row == 1, middle, jnp.where(digit_row == 2, upper, digits))
    digits = digits.astype(jnp.bfloat16)

    def column(row):
        return jnp.broadcast_to(row.astype(jnp.float32), (BLOCK, BLOCK)).T[:, :1]

    all_docs = docs_ref[...].astype(jnp.float32)
    live_columns = column(live_own[...]), column(live_sib[...])
    bounds = []
    for half in range(2):
        block = chip if half == 0 else 15 - chip
        swapped = core if half == 0 else 1 - core
        own_docs = column(docs_ref[:, pl.ds(pl.multiple_of(block * BLOCK, BLOCK), BLOCK)])
        own_docs = jnp.where(
            swapped == 1, jnp.concatenate([own_docs[64:], own_docs[:64]], axis=0), own_docs
        )
        below = jnp.where(all_docs < own_docs, 1.0, 0.0)
        low_bound = jnp.sum(below, axis=1, keepdims=True)
        tiles = (block * BLOCK + BLOCK - jnp.min(low_bound).astype(jnp.int32) + TILE - 1) >> 8
        row = lax.broadcasted_iota(jnp.int32, (BLOCK, 1), 0)
        own_pos = block * BLOCK + ((row + 64 * swapped) & (BLOCK - 1))
        live = jnp.concatenate(
            [col[half * 64 : half * 64 + 64] for col in live_columns], axis=0
        )
        bounds.append((tiles, low_bound.astype(jnp.int32), own_pos, live))

    for group in range(GROUPS):
        dkt_ref[...] = jnp.zeros_like(dkt_ref)
        dvt_ref[...] = jnp.zeros_like(dvt_ref)
        for half in range(2):
            tiles, low_bound, own_pos, live = bounds[half]
            end = ((chip if half == 0 else 15 - chip) + 1) * BLOCK
            rows = slice(half * 64, half * 64 + 64)
            dq_rows = slice(BLOCK + half * 64, BLOCK + half * 64 + 64)

            def columns(head):
                return slice((group * FOLD + head) * HEAD, (group * FOLD + head + 1) * HEAD)

            def from_columns(head):
                start = core * (GROUPS * FOLD * HEAD) + (group * FOLD + head) * HEAD
                return pl.ds(pl.multiple_of(start, HEAD), HEAD)

            for head in range(FOLD):
                q_ref[head * BLOCK : head * BLOCK + 64, :] = q_own[rows, from_columns(head)]
                q_ref[head * BLOCK + 64 : (head + 1) * BLOCK, :] = q_sib[rows, from_columns(head)]

            def key_rows(j):
                return pl.ds(pl.multiple_of(end - TILE * (j + 1) + BLOCK, BLOCK), TILE)

            def tile_columns(j):
                return pl.ds(pl.multiple_of(j * TILE, TILE), TILE)

            def over_tiles(body):
                body(0, True)

                @pl.loop(1, tiles)
                def _(j):
                    body(j, False)

            def score_tile(j, first_tile):
                first = end - TILE * (j + 1)
                key_pos = first + lax.broadcasted_iota(jnp.int32, (BLOCK, TILE), 1)
                bias = jnp.where((key_pos >= low_bound) & (key_pos <= own_pos), 0.0, MASKED)
                scores = dot(q_ref[...], k_nat[group, key_rows(j), :], NT)
                scores = (
                    scores.reshape(FOLD, BLOCK, TILE) * SCALE_LOG2E + bias[None]
                ).reshape(ROWS, TILE)
                s_ref[:, tile_columns(j)] = scores
                peak = jnp.maximum(scores[:, :HEAD], scores[:, HEAD:])
                m_ref[...] = peak if first_tile else jnp.maximum(m_ref[...], peak)

            over_tiles(score_tile)
            m_ref[...] = jnp.broadcast_to(
                jnp.max(m_ref[...], axis=1, keepdims=True), (ROWS, HEAD)
            )

            def weight_tile(j, first_tile):
                peak = m_ref[...]
                scores = s_ref[:, tile_columns(j)]
                left = jnp.exp2(scores[:, :HEAD] - peak)
                right = jnp.exp2(scores[:, HEAD:] - peak)
                weights = jnp.concatenate([left, right], axis=1).astype(jnp.bfloat16)
                p_ref[:, tile_columns(j)] = weights
                part = dot(weights, v_nat[group, key_rows(j), :])
                o_ref[...] = part if first_tile else o_ref[...] + part

            over_tiles(weight_tile)
            for head in range(FOLD):
                span = slice(head * BLOCK, (head + 1) * BLOCK)
                inverse = 1.0 / o_ref[span, HEAD:]
                out = (o_ref[span, :HEAD] * inverse).astype(jnp.bfloat16)
                o_own[rows, columns(head)] = out[:64]
                sib_out[rows, columns(head)] = out[64:]
                cot = jnp.concatenate(
                    [c_own[rows, from_columns(head)], c_sib[rows, from_columns(head)]], axis=0
                )
                grad = (cot.astype(jnp.float32) * (live * inverse)).astype(jnp.bfloat16)
                do_ref[span, :] = grad
                m_ref[span, :] = jnp.broadcast_to(
                    jnp.sum(
                        grad.astype(jnp.float32) * out.astype(jnp.float32), axis=1, keepdims=True
                    ),
                    (BLOCK, HEAD),
                )
            qt_ref[...] = q_ref[...].T
            dot_ref[...] = do_ref[...].T

            def gradient_tile(j, first_tile):
                delta = m_ref[...]
                pushes = dot(do_ref[...], v_nat[group, key_rows(j), :HEAD], NT)
                weights = p_ref[:, tile_columns(j)]
                wide = weights.astype(jnp.float32)
                slopes = jnp.concatenate(
                    [
                        wide[:, :HEAD] * (pushes[:, :HEAD] - delta),
                        wide[:, HEAD:] * (pushes[:, HEAD:] - delta),
                    ],
                    axis=1,
                ).astype(jnp.bfloat16)
                part = dot(slopes, k_nat[group, key_rows(j), :])
                dq_ref[...] = part if first_tile else dq_ref[...] + part
                dkt_ref[:, key_rows(j)] += dot(qt_ref[...], slopes)
                dvt_ref[:, key_rows(j)] += dot(dot_ref[...], weights)

            over_tiles(gradient_tile)
            for head in range(FOLD):
                span = slice(head * BLOCK, (head + 1) * BLOCK)
                out = (dq_ref[span, :] * SCALE).astype(jnp.bfloat16)
                dq_own[rows, columns(head)] = out[:64]
                sib_out[dq_rows, columns(head)] = out[64:]
        for at, term in enumerate(terms):
            low = lows[at]
            if group == 0:
                term[2 * GROUPS * HEAD :, :] = digits
            for half in range(2):
                block = low if half == 0 else 15 - low
                place = pl.ds(pl.multiple_of((block + 1) * BLOCK, BLOCK), BLOCK)
                lanes = slice(half * BLOCK, (half + 1) * BLOCK)
                term[group * HEAD : (group + 1) * HEAD, lanes] = (
                    dkt_ref[:, place] * SCALE
                ).astype(jnp.bfloat16)
                term[(GROUPS + group) * HEAD : (GROUPS + group + 1) * HEAD, lanes] = dvt_ref[
                    :, place
                ].astype(jnp.bfloat16)


def attention(me, count, docs, live_own, live_sib, q_own, q_sib, c_own, c_sib, chunks, interpret=False):
    vmem = pl.BlockSpec(memory_space=pltpu.VMEM)
    half_rows = jax.ShapeDtypeStruct((128, GROUPS * FOLD * HEAD), jnp.bfloat16)
    both_rows = jax.ShapeDtypeStruct((256, GROUPS * FOLD * HEAD), jnp.bfloat16)
    term = jax.ShapeDtypeStruct((TERM_ROWS, 2 * BLOCK), jnp.bfloat16)
    padded = 2048 + BLOCK
    most = 5
    return pl.pallas_call(
        attention_kernel,
        out_shape=(half_rows, half_rows, both_rows) + (term,) * 8,
        in_specs=[pl.BlockSpec(memory_space=pltpu.SMEM)] + [vmem] * 16,
        out_specs=(vmem,) * 11,
        scratch_shapes=[
            pltpu.VMEM((GROUPS, padded, HEAD), jnp.bfloat16),
            pltpu.VMEM((GROUPS, padded, 2 * HEAD), jnp.bfloat16),
            pltpu.VMEM((ROWS, most * TILE), jnp.float32),
            pltpu.VMEM((ROWS, most * TILE), jnp.bfloat16),
            pltpu.VMEM((ROWS, HEAD), jnp.bfloat16),
            pltpu.VMEM((ROWS, HEAD), jnp.bfloat16),
            pltpu.VMEM((HEAD, ROWS), jnp.bfloat16),
            pltpu.VMEM((HEAD, ROWS), jnp.bfloat16),
            pltpu.VMEM((ROWS, HEAD), jnp.float32),
            pltpu.VMEM((ROWS, 2 * HEAD), jnp.float32),
            pltpu.VMEM((ROWS, HEAD), jnp.float32),
            pltpu.VMEM((HEAD, padded), jnp.float32),
            pltpu.VMEM((HEAD, padded), jnp.float32),
        ],
        compiler_params=pltpu.CompilerParams(vmem_limit_bytes=28 * 1024 * 1024),
        cost_estimate=pl.CostEstimate(
            flops=6_000_000_000, bytes_accessed=8_000_000, transcendentals=4_000_000
        ),
        interpret=interpret,
    )(me, count, docs, live_own, live_sib, q_own, q_sib, c_own, c_sib, *chunks)


def closing_kernel(me_ref, *refs):
    terms, (kept, sent, ratio) = refs[:4], refs[4:]
    total = sum(term[...].astype(jnp.float32) for term in terms)
    width = 2 * GROUPS * HEAD
    digits = total[width : width + 8, :HEAD]
    count = digits[0:1] + DIGIT * (digits[1:2] + DIGIT * digits[2:3])
    ratio_row = 32768.0 / count
    ratio[...] = jnp.broadcast_to(ratio_row, (8, HEAD))
    rows = (total[:width] * ratio_row[:, :1]).T
    outer = jnp.concatenate([rows[:64], rows[192:]], axis=0).astype(jnp.bfloat16)
    inner = rows[64:192].astype(jnp.bfloat16)
    first = (me_ref[0] & 1) == 0
    kept[...] = jnp.where(first, outer, inner)
    sent[...] = jnp.where(first, inner, outer)


def closing(me, terms):
    vmem = pl.BlockSpec(memory_space=pltpu.VMEM)
    rows = jax.ShapeDtypeStruct((BLOCK, 2 * GROUPS * HEAD), jnp.bfloat16)
    return pl.pallas_call(
        closing_kernel,
        out_shape=(rows, rows, jax.ShapeDtypeStruct((8, HEAD), jnp.float32)),
        in_specs=[pl.BlockSpec(memory_space=pltpu.SMEM)] + [vmem] * 4,
        out_specs=(vmem,) * 3,
        compiler_params=pltpu.CompilerParams(vmem_limit_bytes=8 * 1024 * 1024),
        cost_estimate=pl.CostEstimate(flops=1_000_000, bytes_accessed=1_000_000, transcendentals=0),
    )(me, *terms)


def scale_kernel(me_ref, ratio, own, got, out):
    at = pl.program_id(0)
    mine = (at >> 1) == (me_ref[0] & 1)
    columns = pl.ds(pl.multiple_of((at & 1) * 1024, 1024), 1024)
    factor = ratio[0:1, 0:1]

    @pl.when(mine)
    def _():
        out[...] = (own[:, columns].astype(jnp.float32) * factor).astype(jnp.bfloat16)

    @pl.when(jnp.logical_not(mine))
    def _():
        out[...] = (got[BLOCK:, columns].astype(jnp.float32) * factor).astype(jnp.bfloat16)


def scaled(me, ratio, own, got):
    vmem = pl.BlockSpec(memory_space=pltpu.VMEM)
    return pl.pallas_call(
        scale_kernel,
        grid=(4,),
        out_shape=jax.ShapeDtypeStruct((BLOCK, 4096), jnp.bfloat16),
        in_specs=[pl.BlockSpec(memory_space=pltpu.SMEM)] + [vmem] * 3,
        out_specs=pl.BlockSpec((BLOCK, 1024), lambda i: (0, i)),
        compiler_params=pltpu.CompilerParams(vmem_limit_bytes=8 * 1024 * 1024),
        cost_estimate=pl.CostEstimate(flops=1_000_000, bytes_accessed=2_000_000, transcendentals=0),
    )(me, ratio, own, got)


def join_kernel(me_ref, kept, got, keys, values):
    first = (me_ref[0] & 1) == 0
    width = GROUPS * HEAD
    for at, out in enumerate((keys, values)):
        columns = slice(at * width, (at + 1) * width)
        own, other = kept[:, columns], got[:, columns]
        out[:, :width] = jnp.where(first, own, other)
        out[:, width:] = jnp.where(first, other, own)


def joined(me, kept, got):
    vmem = pl.BlockSpec(memory_space=pltpu.VMEM)
    whole = pl.BlockSpec((BLOCK, 2 * GROUPS * HEAD), lambda i: (0, 0))
    rows = jax.ShapeDtypeStruct((BLOCK, 2 * GROUPS * HEAD), jnp.bfloat16)
    return pl.pallas_call(
        join_kernel,
        grid=(1,),
        out_shape=(rows, rows),
        in_specs=[pl.BlockSpec(memory_space=pltpu.SMEM)] + [vmem] * 2,
        out_specs=(whole, whole),
        compiler_params=pltpu.CompilerParams(vmem_limit_bytes=4 * 1024 * 1024),
        cost_estimate=pl.CostEstimate(flops=100_000, bytes_accessed=500_000, transcendentals=0),
    )(me, kept, got)


def on_device(queries, keys, values, cotangent, live, docs):
    me = lax.axis_index("ctx")
    core = me % 2

    def move(shift):
        return [(i, (i + shift) % 16) for i in range(16)]

    def swap(bit):
        return [(i, i ^ bit) for i in range(16)]

    def to_right(a):
        return lax.ppermute(a, "ctx", move(4))

    def to_left(a):
        return lax.ppermute(a, "ctx", move(-4))

    def to_side(a):
        return lax.ppermute(a, "ctx", swap(2))

    def to_core(a):
        return lax.ppermute(a, "ctx", swap(1))

    kv_width = GROUPS * HEAD
    q_width = GROUPS * FOLD * HEAD
    keys_got, values_got = to_core(keys[0]), to_core(values[0])
    q_got, c_got = to_core(queries[0]), to_core(cotangent[0])

    def groups(a, b):
        chosen = [jnp.where(core == 0, x[:, :kv_width], x[:, kv_width:]) for x in (a, b)]
        return jnp.concatenate(chosen, axis=1)

    kv_keep, kv_got = groups(keys[0], values[0]), groups(keys_got, values_got)
    first = jnp.where(core == 0, kv_keep, kv_got)
    second = jnp.where(core == 0, kv_got, kv_keep)
    mine = jnp.concatenate([first[:64], second[:64], second[64:], first[64:]], axis=0)

    live_got = to_core(live)
    count = live + live_got
    for bit in (1, 2):
        count = count + lax.ppermute(count, "dp", swap(bit))

    from_left = to_right(mine)
    from_right = to_left(mine)
    beside = to_side(mine)
    beside, from_left, from_right, count = lax.optimization_barrier(
        (beside, from_left, from_right, count)
    )
    beside_left = to_right(beside)
    beside_right = to_left(beside)
    opposite = to_right(from_left)
    beside_opposite = to_left(beside_right)
    count = count + lax.ppermute(count, "dp", swap(8))
    count, _, _ = lax.optimization_barrier((count, beside_left, beside_right))
    count = count + lax.ppermute(count, "dp", swap(6))
    chunks = (
        mine,
        beside,
        from_right,
        beside_right,
        from_left,
        beside_left,
        opposite,
        beside_opposite,
    )

    device = me.reshape(1).astype(jnp.int32)
    results = attention(
        device,
        count,
        docs,
        live,
        live_got,
        queries[0],
        q_got,
        cotangent[0],
        c_got,
        chunks,
    )
    o_own, dq_own, sib_out = results[:3]
    sib_got = to_core(sib_out)
    t_mine, t_beside, t_right, t_beside_right, t_left, t_beside_left, t_opp, t_beside_opp = (
        results[3:]
    )

    def add(*terms):
        return sum(t.astype(jnp.float32) for t in terms).astype(jnp.bfloat16)

    opp_via_right = to_right(t_opp)
    opp_via_left = to_left(t_beside_opp)
    got_beside_1 = to_right(t_beside_right)
    right_sum, left_sum = add(t_right, opp_via_right), add(t_beside_left, opp_via_left)
    got_mine_2 = to_right(right_sum)
    got_beside_2 = to_left(left_sum)
    got_mine_1 = to_left(t_left)
    beside_sum = add(t_beside, got_beside_1, got_beside_2)
    got_side = to_side(beside_sum)
    def join(own, got, width):
        low = jnp.where(core == 0, own, got)
        high = jnp.where(core == 0, got, own)
        return jnp.concatenate([low, high], axis=1)

    attended = join(o_own, sib_got[:BLOCK], q_width)[None]
    t_mine, attended = lax.optimization_barrier((t_mine, attended))
    kept, sent, ratio = closing(device, (t_mine, got_mine_1, got_mine_2, got_side))
    got = to_core(sent)

    grad_queries = scaled(device, ratio, dq_own, sib_got)[None]
    got, grad_queries = lax.optimization_barrier((got, grad_queries))
    key_gradient, value_gradient = joined(device, kept, got)
    return attended, grad_queries, key_gradient[None], value_gradient[None]


def solution(mesh):
    rows = P("dp", "ctx", None)
    return jax.shard_map(
        on_device,
        mesh=mesh,
        in_specs=(rows, rows, rows, rows, P("dp", "ctx"), P("dp", None)),
        out_specs=(rows, rows, rows, rows),
        check_vma=False,
    )
```

```python
from functools import partial
import math

import jax
import jax.numpy as jnp
from jax import lax
from jax.experimental import pallas as pl
from jax.experimental.pallas import tpu as pltpu
from jax.sharding import PartitionSpec as P

HEAD = 128
BLOCK = 128
TILE = 256
GROUPS = 2
FOLD = 8
ROWS = FOLD * BLOCK
MASKED = -1e30
SCALE = 1.0 / math.sqrt(HEAD)
SCALE_LOG2E = SCALE * math.log2(math.e)

TERM_ROWS = 2 * GROUPS * HEAD + 16
DIGIT = 32

NT = (((1,), (1,)), ((), ()))
NN = (((1,), (0,)), ((), ()))


def dot(a, b, dims=NN):
    return lax.dot_general(a, b, dims, preferred_element_type=jnp.float32)


def attention_kernel(
    me_ref,
    count_ref,
    docs_ref,
    live_own,
    live_sib,
    q_own,
    q_sib,
    c_own,
    c_sib,
    *refs,
):
    chips = 8
    chunks = refs[:chips]
    o_own, dq_own, sib_out = refs[chips : chips + 3]
    terms = refs[chips + 3 : 2 * chips + 3]
    (
        k_nat,
        v_nat,
        s_ref,
        p_ref,
        q_ref,
        do_ref,
        qt_ref,
        dot_ref,
        m_ref,
        o_ref,
        dq_ref,
        dkt_ref,
        dvt_ref,
    ) = refs[2 * chips + 3 :]

    me = me_ref[0]
    core, chip = me & 1, me >> 1
    line, side = chip >> 1, chip & 1
    lows = []
    for step in (0, 1, 3, 2):
        for other in range(2):
            lows.append(2 * ((line + step) & 3) + (side ^ other))

    for group in range(GROUPS):
        k_nat[group, 0:BLOCK, :] = jnp.zeros((BLOCK, HEAD), jnp.bfloat16)
        v_nat[group, 0:BLOCK, :HEAD] = jnp.zeros((BLOCK, HEAD), jnp.bfloat16)
        v_nat[group, :, HEAD:] = jnp.ones((v_nat.shape[1], HEAD), jnp.bfloat16)
    for at, chunk in enumerate(chunks):
        low = lows[at]
        for half in range(2):
            block = low if half == 0 else 15 - low
            place = pl.ds(pl.multiple_of((block + 1) * BLOCK, BLOCK), BLOCK)
            rows = slice(half * BLOCK, (half + 1) * BLOCK)
            for group in range(GROUPS):
                k_nat[group, place, :] = chunk[rows, group * HEAD : (group + 1) * HEAD]
                v_nat[group, place, :HEAD] = chunk[
                    rows, (GROUPS + group) * HEAD : (GROUPS + group + 1) * HEAD
                ]

    count = jnp.sum(count_ref[...].astype(jnp.float32), axis=1, keepdims=True)
    upper = jnp.floor(count * (1.0 / (DIGIT * DIGIT)))
    rest = count - upper * (DIGIT * DIGIT)
    middle = jnp.floor(rest * (1.0 / DIGIT))
    digit_row = lax.broadcasted_iota(jnp.int32, (16, 2 * BLOCK), 0)
    digits = jnp.where(digit_row == 0, rest - middle * DIGIT, 0.0)
    digits = jnp.where(digit_row == 1, middle, jnp.where(digit_row == 2, upper, digits))
    digits = digits.astype(jnp.bfloat16)

    def column(row):
        return jnp.broadcast_to(row.astype(jnp.float32), (BLOCK, BLOCK)).T[:, :1]

    all_docs = docs_ref[...].astype(jnp.float32)
    live_columns = column(live_own[...]), column(live_sib[...])
    bounds = []
    for half in range(2):
        block = chip if half == 0 else 15 - chip
        swapped = core if half == 0 else 1 - core
        own_docs = column(docs_ref[:, pl.ds(pl.multiple_of(block * BLOCK, BLOCK), BLOCK)])
        own_docs = jnp.where(
            swapped == 1, jnp.concatenate([own_docs[64:], own_docs[:64]], axis=0), own_docs
        )
        below = jnp.where(all_docs < own_docs, 1.0, 0.0)
        low_bound = jnp.sum(below, axis=1, keepdims=True)
        tiles = (block * BLOCK + BLOCK - jnp.min(low_bound).astype(jnp.int32) + TILE - 1) >> 8
        row = lax.broadcasted_iota(jnp.int32, (BLOCK, 1), 0)
        own_pos = block * BLOCK + ((row + 64 * swapped) & (BLOCK - 1))
        live = jnp.concatenate(
            [col[half * 64 : half * 64 + 64] for col in live_columns], axis=0
        )
        bounds.append((tiles, low_bound.astype(jnp.int32), own_pos, live))

    for group in range(GROUPS):
        dkt_ref[...] = jnp.zeros_like(dkt_ref)
        dvt_ref[...] = jnp.zeros_like(dvt_ref)
        for half in range(2):
            tiles, low_bound, own_pos, live = bounds[half]
            end = ((chip if half == 0 else 15 - chip) + 1) * BLOCK
            rows = slice(half * 64, half * 64 + 64)
            dq_rows = slice(BLOCK + half * 64, BLOCK + half * 64 + 64)

            def columns(head):
                return slice((group * FOLD + head) * HEAD, (group * FOLD + head + 1) * HEAD)

            def from_columns(head):
                start = core * (GROUPS * FOLD * HEAD) + (group * FOLD + head) * HEAD
                return pl.ds(pl.multiple_of(start, HEAD), HEAD)

            for head in range(FOLD):
                q_ref[head * BLOCK : head * BLOCK + 64, :] = q_own[rows, from_columns(head)]
                q_ref[head * BLOCK + 64 : (head + 1) * BLOCK, :] = q_sib[rows, from_columns(head)]

            def key_rows(j):
                return pl.ds(pl.multiple_of(end - TILE * (j + 1) + BLOCK, BLOCK), TILE)

            def tile_columns(j):
                return pl.ds(pl.multiple_of(j * TILE, TILE), TILE)

            def over_tiles(body):
                body(0, True)

                @pl.loop(1, tiles)
                def _(j):
                    body(j, False)

            def score_tile(j, first_tile):
                first = end - TILE * (j + 1)
                key_pos = first + lax.broadcasted_iota(jnp.int32, (BLOCK, TILE), 1)
                bias = jnp.where((key_pos >= low_bound) & (key_pos <= own_pos), 0.0, MASKED)
                scores = dot(q_ref[...], k_nat[group, key_rows(j), :], NT)
                scores = (
                    scores.reshape(FOLD, BLOCK, TILE) * SCALE_LOG2E + bias[None]
                ).reshape(ROWS, TILE)
                s_ref[:, tile_columns(j)] = scores
                peak = jnp.maximum(scores[:, :HEAD], scores[:, HEAD:])
                m_ref[...] = peak if first_tile else jnp.maximum(m_ref[...], peak)

            over_tiles(score_tile)
            m_ref[...] = jnp.broadcast_to(
                jnp.max(m_ref[...], axis=1, keepdims=True), (ROWS, HEAD)
            )

            def weight_tile(j, first_tile):
                peak = m_ref[...]
                scores = s_ref[:, tile_columns(j)]
                left = jnp.exp2(scores[:, :HEAD] - peak)
                right = jnp.exp2(scores[:, HEAD:] - peak)
                weights = jnp.concatenate([left, right], axis=1).astype(jnp.bfloat16)
                p_ref[:, tile_columns(j)] = weights
                part = dot(weights, v_nat[group, key_rows(j), :])
                o_ref[...] = part if first_tile else o_ref[...] + part

            over_tiles(weight_tile)
            for head in range(FOLD):
                span = slice(head * BLOCK, (head + 1) * BLOCK)
                inverse = 1.0 / o_ref[span, HEAD:]
                out = (o_ref[span, :HEAD] * inverse).astype(jnp.bfloat16)
                o_own[rows, columns(head)] = out[:64]
                sib_out[rows, columns(head)] = out[64:]
                cot = jnp.concatenate(
                    [c_own[rows, from_columns(head)], c_sib[rows, from_columns(head)]], axis=0
                )
                grad = (cot.astype(jnp.float32) * (live * inverse)).astype(jnp.bfloat16)
                do_ref[span, :] = grad
                m_ref[span, :] = jnp.broadcast_to(
                    jnp.sum(
                        grad.astype(jnp.float32) * out.astype(jnp.float32), axis=1, keepdims=True
                    ),
                    (BLOCK, HEAD),
                )
            qt_ref[...] = q_ref[...].T
            dot_ref[...] = do_ref[...].T

            def gradient_tile(j, first_tile):
                delta = m_ref[...]
                pushes = dot(do_ref[...], v_nat[group, key_rows(j), :HEAD], NT)
                weights = p_ref[:, tile_columns(j)]
                wide = weights.astype(jnp.float32)
                slopes = jnp.concatenate(
                    [
                        wide[:, :HEAD] * (pushes[:, :HEAD] - delta),
                        wide[:, HEAD:] * (pushes[:, HEAD:] - delta),
                    ],
                    axis=1,
                ).astype(jnp.bfloat16)
                part = dot(slopes, k_nat[group, key_rows(j), :])
                dq_ref[...] = part if first_tile else dq_ref[...] + part
                dkt_ref[:, key_rows(j)] += dot(qt_ref[...], slopes)
                dvt_ref[:, key_rows(j)] += dot(dot_ref[...], weights)

            over_tiles(gradient_tile)
            for head in range(FOLD):
                span = slice(head * BLOCK, (head + 1) * BLOCK)
                out = (dq_ref[span, :] * SCALE).astype(jnp.bfloat16)
                dq_own[rows, columns(head)] = out[:64]
                sib_out[dq_rows, columns(head)] = out[64:]
        for at, term in enumerate(terms):
            low = lows[at]
            if group == 0:
                term[2 * GROUPS * HEAD :, :] = digits
            for half in range(2):
                block = low if half == 0 else 15 - low
                place = pl.ds(pl.multiple_of((block + 1) * BLOCK, BLOCK), BLOCK)
                lanes = slice(half * BLOCK, (half + 1) * BLOCK)
                term[group * HEAD : (group + 1) * HEAD, lanes] = (
                    dkt_ref[:, place] * SCALE
                ).astype(jnp.bfloat16)
                term[(GROUPS + group) * HEAD : (GROUPS + group + 1) * HEAD, lanes] = dvt_ref[
                    :, place
                ].astype(jnp.bfloat16)


def attention(me, count, docs, live_own, live_sib, q_own, q_sib, c_own, c_sib, chunks, interpret=False):
    vmem = pl.BlockSpec(memory_space=pltpu.VMEM)
    half_rows = jax.ShapeDtypeStruct((128, GROUPS * FOLD * HEAD), jnp.bfloat16)
    both_rows = jax.ShapeDtypeStruct((256, GROUPS * FOLD * HEAD), jnp.bfloat16)
    term = jax.ShapeDtypeStruct((TERM_ROWS, 2 * BLOCK), jnp.bfloat16)
    padded = 2048 + BLOCK
    most = 5
    return pl.pallas_call(
        attention_kernel,
        out_shape=(half_rows, half_rows, both_rows) + (term,) * 8,
        in_specs=[pl.BlockSpec(memory_space=pltpu.SMEM)] + [vmem] * 16,
        out_specs=(vmem,) * 11,
        scratch_shapes=[
            pltpu.VMEM((GROUPS, padded, HEAD), jnp.bfloat16),
            pltpu.VMEM((GROUPS, padded, 2 * HEAD), jnp.bfloat16),
            pltpu.VMEM((ROWS, most * TILE), jnp.float32),
            pltpu.VMEM((ROWS, most * TILE), jnp.bfloat16),
            pltpu.VMEM((ROWS, HEAD), jnp.bfloat16),
            pltpu.VMEM((ROWS, HEAD), jnp.bfloat16),
            pltpu.VMEM((HEAD, ROWS), jnp.bfloat16),
            pltpu.VMEM((HEAD, ROWS), jnp.bfloat16),
            pltpu.VMEM((ROWS, HEAD), jnp.float32),
            pltpu.VMEM((ROWS, 2 * HEAD), jnp.float32),
            pltpu.VMEM((ROWS, HEAD), jnp.float32),
            pltpu.VMEM((HEAD, padded), jnp.float32),
            pltpu.VMEM((HEAD, padded), jnp.float32),
        ],
        compiler_params=pltpu.CompilerParams(vmem_limit_bytes=28 * 1024 * 1024),
        cost_estimate=pl.CostEstimate(
            flops=6_000_000_000, bytes_accessed=8_000_000, transcendentals=4_000_000
        ),
        interpret=interpret,
    )(me, count, docs, live_own, live_sib, q_own, q_sib, c_own, c_sib, *chunks)


def closing_kernel(me_ref, *refs):
    terms, (kept, sent, ratio) = refs[:4], refs[4:]
    total = sum(term[...].astype(jnp.float32) for term in terms)
    width = 2 * GROUPS * HEAD
    digits = total[width : width + 8, :HEAD]
    count = digits[0:1] + DIGIT * (digits[1:2] + DIGIT * digits[2:3])
    ratio_row = 32768.0 / count
    ratio[...] = jnp.broadcast_to(ratio_row, (8, HEAD))
    rows = (total[:width] * ratio_row[:, :1]).T
    outer = jnp.concatenate([rows[:64], rows[192:]], axis=0).astype(jnp.bfloat16)
    inner = rows[64:192].astype(jnp.bfloat16)
    first = (me_ref[0] & 1) == 0
    kept[...] = jnp.where(first, outer, inner)
    sent[...] = jnp.where(first, inner, outer)


def closing(me, terms):
    vmem = pl.BlockSpec(memory_space=pltpu.VMEM)
    rows = jax.ShapeDtypeStruct((BLOCK, 2 * GROUPS * HEAD), jnp.bfloat16)
    return pl.pallas_call(
        closing_kernel,
        out_shape=(rows, rows, jax.ShapeDtypeStruct((8, HEAD), jnp.float32)),
        in_specs=[pl.BlockSpec(memory_space=pltpu.SMEM)] + [vmem] * 4,
        out_specs=(vmem,) * 3,
        compiler_params=pltpu.CompilerParams(vmem_limit_bytes=8 * 1024 * 1024),
        cost_estimate=pl.CostEstimate(flops=1_000_000, bytes_accessed=1_000_000, transcendentals=0),
    )(me, *terms)


def scale_kernel(me_ref, ratio, own, got, out):
    at = pl.program_id(0)
    mine = (at >> 1) == (me_ref[0] & 1)
    columns = pl.ds(pl.multiple_of((at & 1) * 1024, 1024), 1024)
    factor = ratio[0:1, 0:1]

    @pl.when(mine)
    def _():
        out[...] = (own[:, columns].astype(jnp.float32) * factor).astype(jnp.bfloat16)

    @pl.when(jnp.logical_not(mine))
    def _():
        out[...] = (got[BLOCK:, columns].astype(jnp.float32) * factor).astype(jnp.bfloat16)


def scaled(me, ratio, own, got):
    vmem = pl.BlockSpec(memory_space=pltpu.VMEM)
    return pl.pallas_call(
        scale_kernel,
        grid=(4,),
        out_shape=jax.ShapeDtypeStruct((BLOCK, 4096), jnp.bfloat16),
        in_specs=[pl.BlockSpec(memory_space=pltpu.SMEM)] + [vmem] * 3,
        out_specs=pl.BlockSpec((BLOCK, 1024), lambda i: (0, i)),
        compiler_params=pltpu.CompilerParams(vmem_limit_bytes=8 * 1024 * 1024),
        cost_estimate=pl.CostEstimate(flops=1_000_000, bytes_accessed=2_000_000, transcendentals=0),
    )(me, ratio, own, got)


def join_kernel(me_ref, kept, got, keys, values):
    first = (me_ref[0] & 1) == 0
    width = GROUPS * HEAD
    for at, out in enumerate((keys, values)):
        columns = slice(at * width, (at + 1) * width)
        own, other = kept[:, columns], got[:, columns]
        out[:, :width] = jnp.where(first, own, other)
        out[:, width:] = jnp.where(first, other, own)


def joined(me, kept, got):
    vmem = pl.BlockSpec(memory_space=pltpu.VMEM)
    whole = pl.BlockSpec((BLOCK, 2 * GROUPS * HEAD), lambda i: (0, 0))
    rows = jax.ShapeDtypeStruct((BLOCK, 2 * GROUPS * HEAD), jnp.bfloat16)
    return pl.pallas_call(
        join_kernel,
        grid=(1,),
        out_shape=(rows, rows),
        in_specs=[pl.BlockSpec(memory_space=pltpu.SMEM)] + [vmem] * 2,
        out_specs=(whole, whole),
        compiler_params=pltpu.CompilerParams(vmem_limit_bytes=4 * 1024 * 1024),
        cost_estimate=pl.CostEstimate(flops=100_000, bytes_accessed=500_000, transcendentals=0),
    )(me, kept, got)


def on_device(queries, keys, values, cotangent, live, docs):
    me = lax.axis_index("ctx")
    core = me % 2

    def move(shift):
        return [(i, (i + shift) % 16) for i in range(16)]

    def swap(bit):
        return [(i, i ^ bit) for i in range(16)]

    def to_right(a):
        return lax.ppermute(a, "ctx", move(4))

    def to_left(a):
        return lax.ppermute(a, "ctx", move(-4))

    def to_side(a):
        return lax.ppermute(a, "ctx", swap(2))

    def to_core(a):
        return lax.ppermute(a, "ctx", swap(1))

    kv_width = GROUPS * HEAD
    q_width = GROUPS * FOLD * HEAD
    keys_got, values_got = to_core(keys[0]), to_core(values[0])
    q_got, c_got = to_core(queries[0]), to_core(cotangent[0])

    def groups(a, b):
        chosen = [jnp.where(core == 0, x[:, :kv_width], x[:, kv_width:]) for x in (a, b)]
        return jnp.concatenate(chosen, axis=1)

    kv_keep, kv_got = groups(keys[0], values[0]), groups(keys_got, values_got)
    first = jnp.where(core == 0, kv_keep, kv_got)
    second = jnp.where(core == 0, kv_got, kv_keep)
    mine = jnp.concatenate([first[:64], second[:64], second[64:], first[64:]], axis=0)

    live_got = to_core(live)
    count = live + live_got
    for bit in (1, 2):
        count = count + lax.ppermute(count, "dp", swap(bit))

    from_left = to_right(mine)
    from_right = to_left(mine)
    beside = to_side(mine)
    beside, from_left, from_right, count = lax.optimization_barrier(
        (beside, from_left, from_right, count)
    )
    beside_left = to_right(beside)
    beside_right = to_left(beside)
    opposite = to_right(from_left)
    beside_opposite = to_left(beside_right)
    count = count + lax.ppermute(count, "dp", swap(6))
    count, _, _ = lax.optimization_barrier((count, beside_left, beside_right))
    count = count + lax.ppermute(count, "dp", swap(8))
    chunks = (
        mine,
        beside,
        from_right,
        beside_right,
        from_left,
        beside_left,
        opposite,
        beside_opposite,
    )

    device = me.reshape(1).astype(jnp.int32)
    results = attention(
        device,
        count,
        docs,
        live,
        live_got,
        queries[0],
        q_got,
        cotangent[0],
        c_got,
        chunks,
    )
    o_own, dq_own, sib_out = results[:3]
    sib_got = to_core(sib_out)
    t_mine, t_beside, t_right, t_beside_right, t_left, t_beside_left, t_opp, t_beside_opp = (
        results[3:]
    )

    def add(*terms):
        return sum(t.astype(jnp.float32) for t in terms).astype(jnp.bfloat16)

    opp_via_right = to_right(t_opp)
    opp_via_left = to_left(t_beside_opp)
    got_beside_1 = to_right(t_beside_right)
    right_sum, left_sum = add(t_right, opp_via_right), add(t_beside_left, opp_via_left)
    got_mine_2 = to_right(right_sum)
    got_beside_2 = to_left(left_sum)
    got_mine_1 = to_left(t_left)
    beside_sum = add(t_beside, got_beside_1, got_beside_2)
    got_side = to_side(beside_sum)
    def join(own, got, width):
        low = jnp.where(core == 0, own, got)
        high = jnp.where(core == 0, got, own)
        return jnp.concatenate([low, high], axis=1)

    attended = join(o_own, sib_got[:BLOCK], q_width)[None]
    t_mine, attended = lax.optimization_barrier((t_mine, attended))
    kept, sent, ratio = closing(device, (t_mine, got_mine_1, got_mine_2, got_side))
    got = to_core(sent)

    grad_queries = scaled(device, ratio, dq_own, sib_got)[None]
    got, grad_queries = lax.optimization_barrier((got, grad_queries))
    key_gradient, value_gradient = joined(device, kept, got)
    return attended, grad_queries, key_gradient[None], value_gradient[None]


def solution(mesh):
    rows = P("dp", "ctx", None)
    return jax.shard_map(
        on_device,
        mesh=mesh,
        in_specs=(rows, rows, rows, rows, P("dp", "ctx"), P("dp", None)),
        out_specs=(rows, rows, rows, rows),
        check_vma=False,
    )
```

```python
import functools
import math

import jax
import jax.numpy as jnp
from jax import lax
from jax.experimental import pallas as pl
from jax.experimental.pallas import tpu as pltpu
from jax.sharding import PartitionSpec as P

HEAD = 128
BLOCK = 128
TILE = 256
GROUPS = 2
FOLD = 8
ROWS = FOLD * BLOCK
MASKED = -1e30
SCALE = 1.0 / math.sqrt(HEAD)
SCALE_LOG2E = SCALE * math.log2(math.e)

TERM_ROWS = 2 * GROUPS * HEAD + 16
DIGIT = 32

NT = (((1,), (1,)), ((), ()))
NN = (((1,), (0,)), ((), ()))


def dot(a, b, dims=NN):
    return lax.dot_general(a, b, dims, preferred_element_type=jnp.float32)


def attention_kernel(
    me_ref,
    count_ref,
    docs_ref,
    live_own,
    live_sib,
    q_own,
    q_sib,
    c_own,
    c_sib,
    *refs,
):
    chips = 8
    chunks = refs[:chips]
    o_own, dq_own, sib_out = refs[chips : chips + 3]
    terms = refs[chips + 3 : 2 * chips + 3]
    (
        k_nat,
        v_nat,
        s_ref,
        p_ref,
        q_ref,
        do_ref,
        qt_ref,
        dot_ref,
        m_ref,
        o_ref,
        dq_ref,
        dkt_ref,
        dvt_ref,
    ) = refs[2 * chips + 3 :]

    me = me_ref[0]
    core, chip = me & 1, me >> 1
    line, side = chip >> 1, chip & 1
    lows = []
    for step in (0, 1, 3, 2):
        for other in range(2):
            lows.append(2 * ((line + step) & 3) + (side ^ other))

    for group in range(GROUPS):
        k_nat[group, 0:BLOCK, :] = jnp.zeros((BLOCK, HEAD), jnp.bfloat16)
        v_nat[group, 0:BLOCK, :HEAD] = jnp.zeros((BLOCK, HEAD), jnp.bfloat16)
        v_nat[group, :, HEAD:] = jnp.ones((v_nat.shape[1], HEAD), jnp.bfloat16)
    for at, chunk in enumerate(chunks):
        low = lows[at]
        for half in range(2):
            block = low if half == 0 else 15 - low
            place = pl.ds(pl.multiple_of((block + 1) * BLOCK, BLOCK), BLOCK)
            rows = slice(half * BLOCK, (half + 1) * BLOCK)
            for group in range(GROUPS):
                k_nat[group, place, :] = chunk[rows, group * HEAD : (group + 1) * HEAD]
                v_nat[group, place, :HEAD] = chunk[
                    rows, (GROUPS + group) * HEAD : (GROUPS + group + 1) * HEAD
                ]

    count = jnp.sum(count_ref[...].astype(jnp.float32), axis=1, keepdims=True)
    upper = jnp.floor(count * (1.0 / (DIGIT * DIGIT)))
    rest = count - upper * (DIGIT * DIGIT)
    middle = jnp.floor(rest * (1.0 / DIGIT))
    digit_row = lax.broadcasted_iota(jnp.int32, (16, 2 * BLOCK), 0)
    digits = jnp.where(digit_row == 0, rest - middle * DIGIT, 0.0)
    digits = jnp.where(digit_row == 1, middle, jnp.where(digit_row == 2, upper, digits))
    digits = digits.astype(jnp.bfloat16)

    def column(row):
        return jnp.broadcast_to(row.astype(jnp.float32), (BLOCK, BLOCK)).T[:, :1]

    all_docs = docs_ref[...].astype(jnp.float32)
    live_columns = column(live_own[...]), column(live_sib[...])
    bounds = []
    for half in range(2):
        block = chip if half == 0 else 15 - chip
        swapped = core if half == 0 else 1 - core
        own_docs = column(docs_ref[:, pl.ds(pl.multiple_of(block * BLOCK, BLOCK), BLOCK)])
        own_docs = jnp.where(
            swapped == 1, jnp.concatenate([own_docs[64:], own_docs[:64]], axis=0), own_docs
        )
        below = jnp.where(all_docs < own_docs, 1.0, 0.0)
        low_bound = jnp.sum(below, axis=1, keepdims=True)
        seen = (block * BLOCK + 2 * BLOCK - 1 - jnp.min(low_bound).astype(jnp.int32)) >> 7
        tiles = jnp.maximum(seen >> 1, 1)
        tail = (seen & 1) * (seen >> 1)
        row = lax.broadcasted_iota(jnp.int32, (BLOCK, 1), 0)
        own_pos = block * BLOCK + ((row + 64 * swapped) & (BLOCK - 1))
        live = jnp.concatenate(
            [col[half * 64 : half * 64 + 64] for col in live_columns], axis=0
        )
        bounds.append((tiles, tail, low_bound.astype(jnp.int32), own_pos, live))

    for group in range(GROUPS):
        dkt_ref[...] = jnp.zeros_like(dkt_ref)
        dvt_ref[...] = jnp.zeros_like(dvt_ref)
        for half in range(2):
            tiles, tail, low_bound, own_pos, live = bounds[half]
            end = ((chip if half == 0 else 15 - chip) + 1) * BLOCK
            rows = slice(half * 64, half * 64 + 64)
            dq_rows = slice(BLOCK + half * 64, BLOCK + half * 64 + 64)

            def columns(head):
                return slice((group * FOLD + head) * HEAD, (group * FOLD + head + 1) * HEAD)

            def from_columns(head):
                start = core * (GROUPS * FOLD * HEAD) + (group * FOLD + head) * HEAD
                return pl.ds(pl.multiple_of(start, HEAD), HEAD)

            for head in range(FOLD):
                q_ref[head * BLOCK : head * BLOCK + 64, :] = q_own[rows, from_columns(head)]
                q_ref[head * BLOCK + 64 : (head + 1) * BLOCK, :] = q_sib[rows, from_columns(head)]

            def key_rows(j, width):
                return pl.ds(pl.multiple_of(end - TILE * j - width + BLOCK, BLOCK), width)

            def tile_columns(j, width):
                return pl.ds(pl.multiple_of(j * TILE, TILE), width)

            def lanes_of(array):
                return [array[:, at : at + HEAD] for at in range(0, array.shape[1], HEAD)]

            def side_by_side(parts):
                return parts[0] if len(parts) == 1 else jnp.concatenate(parts, axis=1)

            def over_tiles(body):
                body(0, True, TILE)

                @pl.loop(1, tiles)
                def _(j):
                    body(j, False, TILE)

                @pl.when(tail > 0)
                def _():
                    body(tiles, False, BLOCK)

            def score_tile(j, first_tile, width):
                first = end - TILE * j - width
                key_pos = first + lax.broadcasted_iota(jnp.int32, (BLOCK, width), 1)
                bias = jnp.where((key_pos >= low_bound) & (key_pos <= own_pos), 0.0, MASKED)
                scores = dot(q_ref[...], k_nat[group, key_rows(j, width), :], NT)
                scores = (
                    scores.reshape(FOLD, BLOCK, width) * SCALE_LOG2E + bias[None]
                ).reshape(ROWS, width)
                s_ref[:, tile_columns(j, width)] = scores
                peak = functools.reduce(jnp.maximum, lanes_of(scores))
                m_ref[...] = peak if first_tile else jnp.maximum(m_ref[...], peak)

            over_tiles(score_tile)
            m_ref[...] = jnp.broadcast_to(
                jnp.max(m_ref[...], axis=1, keepdims=True), (ROWS, HEAD)
            )

            def weight_tile(j, first_tile, width):
                peak = m_ref[...]
                scores = s_ref[:, tile_columns(j, width)]
                weights = side_by_side(
                    [jnp.exp2(part - peak) for part in lanes_of(scores)]
                ).astype(jnp.bfloat16)
                p_ref[:, tile_columns(j, width)] = weights
                part = dot(weights, v_nat[group, key_rows(j, width), :])
                o_ref[...] = part if first_tile else o_ref[...] + part

            over_tiles(weight_tile)
            for head in range(FOLD):
                span = slice(head * BLOCK, (head + 1) * BLOCK)
                inverse = 1.0 / o_ref[span, HEAD:]
                out = (o_ref[span, :HEAD] * inverse).astype(jnp.bfloat16)
                o_own[rows, columns(head)] = out[:64]
                sib_out[rows, columns(head)] = out[64:]
                cot = jnp.concatenate(
                    [c_own[rows, from_columns(head)], c_sib[rows, from_columns(head)]], axis=0
                )
                grad = (cot.astype(jnp.float32) * (live * inverse)).astype(jnp.bfloat16)
                do_ref[span, :] = grad
                m_ref[span, :] = jnp.broadcast_to(
                    jnp.sum(
                        grad.astype(jnp.float32) * out.astype(jnp.float32), axis=1, keepdims=True
                    ),
                    (BLOCK, HEAD),
                )
            qt_ref[...] = q_ref[...].T
            dot_ref[...] = do_ref[...].T

            def gradient_tile(j, first_tile, width):
                delta = m_ref[...]
                pushes = dot(do_ref[...], v_nat[group, key_rows(j, width), :HEAD], NT)
                weights = p_ref[:, tile_columns(j, width)]
                wide = weights.astype(jnp.float32)
                slopes = side_by_side(
                    [w * (p - delta) for w, p in zip(lanes_of(wide), lanes_of(pushes))]
                ).astype(jnp.bfloat16)
                part = dot(slopes, k_nat[group, key_rows(j, width), :])
                dq_ref[...] = part if first_tile else dq_ref[...] + part
                dkt_ref[:, key_rows(j, width)] += dot(qt_ref[...], slopes)
                dvt_ref[:, key_rows(j, width)] += dot(dot_ref[...], weights)

            over_tiles(gradient_tile)
            for head in range(FOLD):
                span = slice(head * BLOCK, (head + 1) * BLOCK)
                out = (dq_ref[span, :] * SCALE).astype(jnp.bfloat16)
                dq_own[rows, columns(head)] = out[:64]
                sib_out[dq_rows, columns(head)] = out[64:]
        for at, term in enumerate(terms):
            low = lows[at]
            if group == 0:
                term[2 * GROUPS * HEAD :, :] = digits
            for half in range(2):
                block = low if half == 0 else 15 - low
                place = pl.ds(pl.multiple_of((block + 1) * BLOCK, BLOCK), BLOCK)
                lanes = slice(half * BLOCK, (half + 1) * BLOCK)
                term[group * HEAD : (group + 1) * HEAD, lanes] = (
                    dkt_ref[:, place] * SCALE
                ).astype(jnp.bfloat16)
                term[(GROUPS + group) * HEAD : (GROUPS + group + 1) * HEAD, lanes] = dvt_ref[
                    :, place
                ].astype(jnp.bfloat16)


def attention(me, count, docs, live_own, live_sib, q_own, q_sib, c_own, c_sib, chunks, interpret=False):
    vmem = pl.BlockSpec(memory_space=pltpu.VMEM)
    half_rows = jax.ShapeDtypeStruct((128, GROUPS * FOLD * HEAD), jnp.bfloat16)
    both_rows = jax.ShapeDtypeStruct((256, GROUPS * FOLD * HEAD), jnp.bfloat16)
    term = jax.ShapeDtypeStruct((TERM_ROWS, 2 * BLOCK), jnp.bfloat16)
    padded = 2048 + BLOCK
    most = 5
    return pl.pallas_call(
        attention_kernel,
        out_shape=(half_rows, half_rows, both_rows) + (term,) * 8,
        in_specs=[pl.BlockSpec(memory_space=pltpu.SMEM)] + [vmem] * 16,
        out_specs=(vmem,) * 11,
        scratch_shapes=[
            pltpu.VMEM((GROUPS, padded, HEAD), jnp.bfloat16),
            pltpu.VMEM((GROUPS, padded, 2 * HEAD), jnp.bfloat16),
            pltpu.VMEM((ROWS, most * TILE), jnp.float32),
            pltpu.VMEM((ROWS, most * TILE), jnp.bfloat16),
            pltpu.VMEM((ROWS, HEAD), jnp.bfloat16),
            pltpu.VMEM((ROWS, HEAD), jnp.bfloat16),
            pltpu.VMEM((HEAD, ROWS), jnp.bfloat16),
            pltpu.VMEM((HEAD, ROWS), jnp.bfloat16),
            pltpu.VMEM((ROWS, HEAD), jnp.float32),
            pltpu.VMEM((ROWS, 2 * HEAD), jnp.float32),
            pltpu.VMEM((ROWS, HEAD), jnp.float32),
            pltpu.VMEM((HEAD, padded), jnp.float32),
            pltpu.VMEM((HEAD, padded), jnp.float32),
        ],
        compiler_params=pltpu.CompilerParams(vmem_limit_bytes=28 * 1024 * 1024),
        cost_estimate=pl.CostEstimate(
            flops=6_000_000_000, bytes_accessed=8_000_000, transcendentals=4_000_000
        ),
        interpret=interpret,
    )(me, count, docs, live_own, live_sib, q_own, q_sib, c_own, c_sib, *chunks)


def closing_kernel(me_ref, *refs):
    terms, (kept, sent, ratio) = refs[:4], refs[4:]
    total = sum(term[...].astype(jnp.float32) for term in terms)
    width = 2 * GROUPS * HEAD
    digits = total[width : width + 8, :HEAD]
    count = digits[0:1] + DIGIT * (digits[1:2] + DIGIT * digits[2:3])
    ratio_row = 32768.0 / count
    ratio[...] = jnp.broadcast_to(ratio_row, (8, HEAD))
    rows = (total[:width] * ratio_row[:, :1]).T
    outer = jnp.concatenate([rows[:64], rows[192:]], axis=0).astype(jnp.bfloat16)
    inner = rows[64:192].astype(jnp.bfloat16)
    first = (me_ref[0] & 1) == 0
    kept[...] = jnp.where(first, outer, inner)
    sent[...] = jnp.where(first, inner, outer)


def closing(me, terms):
    vmem = pl.BlockSpec(memory_space=pltpu.VMEM)
    rows = jax.ShapeDtypeStruct((BLOCK, 2 * GROUPS * HEAD), jnp.bfloat16)
    return pl.pallas_call(
        closing_kernel,
        out_shape=(rows, rows, jax.ShapeDtypeStruct((8, HEAD), jnp.float32)),
        in_specs=[pl.BlockSpec(memory_space=pltpu.SMEM)] + [vmem] * 4,
        out_specs=(vmem,) * 3,
        compiler_params=pltpu.CompilerParams(vmem_limit_bytes=8 * 1024 * 1024),
        cost_estimate=pl.CostEstimate(flops=1_000_000, bytes_accessed=1_000_000, transcendentals=0),
    )(me, *terms)


def scale_kernel(me_ref, ratio, own, got, out):
    at = pl.program_id(0)
    mine = (at >> 1) == (me_ref[0] & 1)
    columns = pl.ds(pl.multiple_of((at & 1) * 1024, 1024), 1024)
    factor = ratio[0:1, 0:1]

    @pl.when(mine)
    def _():
        out[...] = (own[:, columns].astype(jnp.float32) * factor).astype(jnp.bfloat16)

    @pl.when(jnp.logical_not(mine))
    def _():
        out[...] = (got[BLOCK:, columns].astype(jnp.float32) * factor).astype(jnp.bfloat16)


def scaled(me, ratio, own, got):
    vmem = pl.BlockSpec(memory_space=pltpu.VMEM)
    return pl.pallas_call(
        scale_kernel,
        grid=(4,),
        out_shape=jax.ShapeDtypeStruct((BLOCK, 4096), jnp.bfloat16),
        in_specs=[pl.BlockSpec(memory_space=pltpu.SMEM)] + [vmem] * 3,
        out_specs=pl.BlockSpec((BLOCK, 1024), lambda i: (0, i)),
        compiler_params=pltpu.CompilerParams(vmem_limit_bytes=8 * 1024 * 1024),
        cost_estimate=pl.CostEstimate(flops=1_000_000, bytes_accessed=2_000_000, transcendentals=0),
    )(me, ratio, own, got)


def join_kernel(me_ref, kept, got, keys, values):
    first = (me_ref[0] & 1) == 0
    width = GROUPS * HEAD
    for at, out in enumerate((keys, values)):
        columns = slice(at * width, (at + 1) * width)
        own, other = kept[:, columns], got[:, columns]
        out[:, :width] = jnp.where(first, own, other)
        out[:, width:] = jnp.where(first, other, own)


def joined(me, kept, got):
    vmem = pl.BlockSpec(memory_space=pltpu.VMEM)
    whole = pl.BlockSpec((BLOCK, 2 * GROUPS * HEAD), lambda i: (0, 0))
    rows = jax.ShapeDtypeStruct((BLOCK, 2 * GROUPS * HEAD), jnp.bfloat16)
    return pl.pallas_call(
        join_kernel,
        grid=(1,),
        out_shape=(rows, rows),
        in_specs=[pl.BlockSpec(memory_space=pltpu.SMEM)] + [vmem] * 2,
        out_specs=(whole, whole),
        compiler_params=pltpu.CompilerParams(vmem_limit_bytes=4 * 1024 * 1024),
        cost_estimate=pl.CostEstimate(flops=100_000, bytes_accessed=500_000, transcendentals=0),
    )(me, kept, got)


def on_device(queries, keys, values, cotangent, live, docs):
    me = lax.axis_index("ctx")
    core = me % 2

    def move(shift):
        return [(i, (i + shift) % 16) for i in range(16)]

    def swap(bit):
        return [(i, i ^ bit) for i in range(16)]

    def to_right(a):
        return lax.ppermute(a, "ctx", move(4))

    def to_left(a):
        return lax.ppermute(a, "ctx", move(-4))

    def to_side(a):
        return lax.ppermute(a, "ctx", swap(2))

    def to_core(a):
        return lax.ppermute(a, "ctx", swap(1))

    kv_width = GROUPS * HEAD
    q_width = GROUPS * FOLD * HEAD
    keys_got, values_got = to_core(keys[0]), to_core(values[0])
    q_got, c_got = to_core(queries[0]), to_core(cotangent[0])

    def groups(a, b):
        chosen = [jnp.where(core == 0, x[:, :kv_width], x[:, kv_width:]) for x in (a, b)]
        return jnp.concatenate(chosen, axis=1)

    kv_keep, kv_got = groups(keys[0], values[0]), groups(keys_got, values_got)
    first = jnp.where(core == 0, kv_keep, kv_got)
    second = jnp.where(core == 0, kv_got, kv_keep)
    mine = jnp.concatenate([first[:64], second[:64], second[64:], first[64:]], axis=0)

    live_got = to_core(live)
    count = live + live_got
    for bit in (1, 2):
        count = count + lax.ppermute(count, "dp", swap(bit))

    from_left = to_right(mine)
    from_right = to_left(mine)
    beside = to_side(mine)
    beside, from_left, from_right, count = lax.optimization_barrier(
        (beside, from_left, from_right, count)
    )
    beside_left = to_right(beside)
    beside_right = to_left(beside)
    opposite = to_right(from_left)
    beside_opposite = to_left(beside_right)
    count = count + lax.ppermute(count, "dp", swap(8))
    count, _, _ = lax.optimization_barrier((count, beside_left, beside_right))
    count = count + lax.ppermute(count, "dp", swap(6))
    chunks = (
        mine,
        beside,
        from_right,
        beside_right,
        from_left,
        beside_left,
        opposite,
        beside_opposite,
    )

    device = me.reshape(1).astype(jnp.int32)
    results = attention(
        device,
        count,
        docs,
        live,
        live_got,
        queries[0],
        q_got,
        cotangent[0],
        c_got,
        chunks,
    )
    o_own, dq_own, sib_out = results[:3]
    sib_got = to_core(sib_out)
    t_mine, t_beside, t_right, t_beside_right, t_left, t_beside_left, t_opp, t_beside_opp = (
        results[3:]
    )

    def add(*terms):
        return sum(t.astype(jnp.float32) for t in terms).astype(jnp.bfloat16)

    opp_via_right = to_right(t_opp)
    opp_via_left = to_left(t_beside_opp)
    got_beside_1 = to_right(t_beside_right)
    right_sum, left_sum = add(t_right, opp_via_right), add(t_beside_left, opp_via_left)
    got_mine_2 = to_right(right_sum)
    got_beside_2 = to_left(left_sum)
    got_mine_1 = to_left(t_left)
    beside_sum = add(t_beside, got_beside_1, got_beside_2)
    got_side = to_side(beside_sum)
    def join(own, got, width):
        low = jnp.where(core == 0, own, got)
        high = jnp.where(core == 0, got, own)
        return jnp.concatenate([low, high], axis=1)

    attended = join(o_own, sib_got[:BLOCK], q_width)[None]
    t_mine, attended = lax.optimization_barrier((t_mine, attended))
    kept, sent, ratio = closing(device, (t_mine, got_mine_1, got_mine_2, got_side))
    got = to_core(sent)

    grad_queries = scaled(device, ratio, dq_own, sib_got)[None]
    got, grad_queries = lax.optimization_barrier((got, grad_queries))
    key_gradient, value_gradient = joined(device, kept, got)
    return attended, grad_queries, key_gradient[None], value_gradient[None]


def solution(mesh):
    rows = P("dp", "ctx", None)
    return jax.shard_map(
        on_device,
        mesh=mesh,
        in_specs=(rows, rows, rows, rows, P("dp", "ctx"), P("dp", None)),
        out_specs=(rows, rows, rows, rows),
        check_vma=False,
    )
```

```python
import functools
import math

import jax
import jax.numpy as jnp
from jax import lax
from jax.experimental import pallas as pl
from jax.experimental.pallas import tpu as pltpu
from jax.sharding import PartitionSpec as P

HEAD = 128
BLOCK = 128
TILE = 256
GROUPS = 2
FOLD = 8
ROWS = FOLD * BLOCK
MASKED = -1e30
SCALE = 1.0 / math.sqrt(HEAD)
SCALE_LOG2E = SCALE * math.log2(math.e)

TERM_ROWS = 2 * GROUPS * HEAD + 16
DIGIT = 32

NT = (((1,), (1,)), ((), ()))
NN = (((1,), (0,)), ((), ()))


def dot(a, b, dims=NN):
    return lax.dot_general(a, b, dims, preferred_element_type=jnp.float32)


def attention_kernel(
    me_ref,
    count_ref,
    docs_ref,
    live_own,
    live_sib,
    q_own,
    q_sib,
    c_own,
    c_sib,
    *refs,
):
    chips = 8
    chunks = refs[:chips]
    o_own, dq_own, sib_out = refs[chips : chips + 3]
    terms = refs[chips + 3 : 2 * chips + 3]
    (
        k_nat,
        v_nat,
        s_ref,
        p_ref,
        q_ref,
        do_ref,
        qt_ref,
        dot_ref,
        m_ref,
        o_ref,
        dq_ref,
        dkt_ref,
        dvt_ref,
    ) = refs[2 * chips + 3 :]

    me = me_ref[0]
    core, chip = me & 1, me >> 1
    line, side = chip >> 1, chip & 1
    lows = []
    for step in (0, 1, 3, 2):
        for other in range(2):
            lows.append(2 * ((line + step) & 3) + (side ^ other))

    for group in range(GROUPS):
        k_nat[group, 0:BLOCK, :] = jnp.zeros((BLOCK, HEAD), jnp.bfloat16)
        v_nat[group, 0:BLOCK, :HEAD] = jnp.zeros((BLOCK, HEAD), jnp.bfloat16)
        v_nat[group, :, HEAD:] = jnp.ones((v_nat.shape[1], HEAD), jnp.bfloat16)
    for at, chunk in enumerate(chunks):
        low = lows[at]
        for half in range(2):
            block = low if half == 0 else 15 - low
            place = pl.ds(pl.multiple_of((block + 1) * BLOCK, BLOCK), BLOCK)
            rows = slice(half * BLOCK, (half + 1) * BLOCK)
            for group in range(GROUPS):
                k_nat[group, place, :] = chunk[rows, group * HEAD : (group + 1) * HEAD]
                v_nat[group, place, :HEAD] = chunk[
                    rows, (GROUPS + group) * HEAD : (GROUPS + group + 1) * HEAD
                ]

    count = jnp.sum(count_ref[...].astype(jnp.float32), axis=1, keepdims=True)
    upper = jnp.floor(count * (1.0 / (DIGIT * DIGIT)))
    rest = count - upper * (DIGIT * DIGIT)
    middle = jnp.floor(rest * (1.0 / DIGIT))
    digit_row = lax.broadcasted_iota(jnp.int32, (16, 2 * BLOCK), 0)
    digits = jnp.where(digit_row == 0, rest - middle * DIGIT, 0.0)
    digits = jnp.where(digit_row == 1, middle, jnp.where(digit_row == 2, upper, digits))
    digits = digits.astype(jnp.bfloat16)

    def column(row):
        return jnp.broadcast_to(row.astype(jnp.float32), (BLOCK, BLOCK)).T[:, :1]

    all_docs = docs_ref[...].astype(jnp.float32)
    live_columns = column(live_own[...]), column(live_sib[...])
    bounds = []
    for half in range(2):
        block = chip if half == 0 else 15 - chip
        swapped = core if half == 0 else 1 - core
        own_docs = column(docs_ref[:, pl.ds(pl.multiple_of(block * BLOCK, BLOCK), BLOCK)])
        own_docs = jnp.where(
            swapped == 1, jnp.concatenate([own_docs[64:], own_docs[:64]], axis=0), own_docs
        )
        below = jnp.where(all_docs < own_docs, 1.0, 0.0)
        low_bound = jnp.sum(below, axis=1, keepdims=True)
        seen = (block * BLOCK + 2 * BLOCK - 1 - jnp.min(low_bound).astype(jnp.int32)) >> 7
        tiles = jnp.maximum(seen >> 1, 1)
        tail = (seen & 1) * (seen >> 1)
        row = lax.broadcasted_iota(jnp.int32, (BLOCK, 1), 0)
        own_pos = block * BLOCK + ((row + 64 * swapped) & (BLOCK - 1))
        live = jnp.concatenate(
            [col[half * 64 : half * 64 + 64] for col in live_columns], axis=0
        )
        bounds.append((tiles, tail, low_bound.astype(jnp.int32), own_pos, live))

    for group in range(GROUPS):
        dkt_ref[...] = jnp.zeros_like(dkt_ref)
        dvt_ref[...] = jnp.zeros_like(dvt_ref)
        for half in range(2):
            tiles, tail, low_bound, own_pos, live = bounds[half]
            end = ((chip if half == 0 else 15 - chip) + 1) * BLOCK
            rows = slice(half * 64, half * 64 + 64)
            dq_rows = slice(BLOCK + half * 64, BLOCK + half * 64 + 64)

            def columns(head):
                return slice((group * FOLD + head) * HEAD, (group * FOLD + head + 1) * HEAD)

            def from_columns(head):
                start = core * (GROUPS * FOLD * HEAD) + (group * FOLD + head) * HEAD
                return pl.ds(pl.multiple_of(start, HEAD), HEAD)

            for head in range(FOLD):
                q_ref[head * BLOCK : head * BLOCK + 64, :] = q_own[rows, from_columns(head)]
                q_ref[head * BLOCK + 64 : (head + 1) * BLOCK, :] = q_sib[rows, from_columns(head)]

            def key_rows(j, width):
                return pl.ds(pl.multiple_of(end - TILE * j - width + BLOCK, BLOCK), width)

            def tile_columns(j, width):
                return pl.ds(pl.multiple_of(j * TILE, TILE), width)

            def lanes_of(array):
                return [array[:, at : at + HEAD] for at in range(0, array.shape[1], HEAD)]

            def side_by_side(parts):
                return parts[0] if len(parts) == 1 else jnp.concatenate(parts, axis=1)

            def over_tiles(body):
                body(0, True, TILE)

                @pl.loop(1, tiles)
                def _(j):
                    body(j, False, TILE)

                @pl.when(tail > 0)
                def _():
                    body(tiles, False, BLOCK)

            def score_tile(j, first_tile, width):
                first = end - TILE * j - width
                key_pos = first + lax.broadcasted_iota(jnp.int32, (BLOCK, width), 1)
                bias = jnp.where((key_pos >= low_bound) & (key_pos <= own_pos), 0.0, MASKED)
                scores = dot(q_ref[...], k_nat[group, key_rows(j, width), :], NT)
                scores = (
                    scores.reshape(FOLD, BLOCK, width) * SCALE_LOG2E + bias[None]
                ).reshape(ROWS, width)
                s_ref[:, tile_columns(j, width)] = scores
                peak = functools.reduce(jnp.maximum, lanes_of(scores))
                m_ref[...] = peak if first_tile else jnp.maximum(m_ref[...], peak)

            over_tiles(score_tile)
            m_ref[...] = jnp.broadcast_to(
                jnp.max(m_ref[...], axis=1, keepdims=True), (ROWS, HEAD)
            )

            def weight_tile(j, first_tile, width):
                peak = m_ref[...]
                scores = s_ref[:, tile_columns(j, width)]
                weights = side_by_side(
                    [jnp.exp2(part - peak) for part in lanes_of(scores)]
                ).astype(jnp.bfloat16)
                p_ref[:, tile_columns(j, width)] = weights
                part = dot(weights, v_nat[group, key_rows(j, width), :])
                o_ref[...] = part if first_tile else o_ref[...] + part

            over_tiles(weight_tile)
            for head in range(FOLD):
                span = slice(head * BLOCK, (head + 1) * BLOCK)
                inverse = 1.0 / o_ref[span, HEAD:]
                out = (o_ref[span, :HEAD] * inverse).astype(jnp.bfloat16)
                o_own[rows, columns(head)] = out[:64]
                sib_out[rows, columns(head)] = out[64:]
                cot = jnp.concatenate(
                    [c_own[rows, from_columns(head)], c_sib[rows, from_columns(head)]], axis=0
                )
                grad = (cot.astype(jnp.float32) * (live * inverse)).astype(jnp.bfloat16)
                do_ref[span, :] = grad
                m_ref[span, :] = jnp.broadcast_to(
                    jnp.sum(
                        grad.astype(jnp.float32) * out.astype(jnp.float32), axis=1, keepdims=True
                    ),
                    (BLOCK, HEAD),
                )
            qt_ref[...] = q_ref[...].T
            dot_ref[...] = do_ref[...].T

            def gradient_tile(j, first_tile, width):
                delta = m_ref[...]
                pushes = dot(do_ref[...], v_nat[group, key_rows(j, width), :HEAD], NT)
                weights = p_ref[:, tile_columns(j, width)]
                wide = weights.astype(jnp.float32)
                slopes = side_by_side(
                    [w * (p - delta) for w, p in zip(lanes_of(wide), lanes_of(pushes))]
                ).astype(jnp.bfloat16)
                part = dot(slopes, k_nat[group, key_rows(j, width), :])
                dq_ref[...] = part if first_tile else dq_ref[...] + part
                dkt_ref[:, key_rows(j, width)] += dot(qt_ref[...], slopes)
                dvt_ref[:, key_rows(j, width)] += dot(dot_ref[...], weights)

            over_tiles(gradient_tile)
            for head in range(FOLD):
                span = slice(head * BLOCK, (head + 1) * BLOCK)
                out = (dq_ref[span, :] * SCALE).astype(jnp.bfloat16)
                dq_own[rows, columns(head)] = out[:64]
                sib_out[dq_rows, columns(head)] = out[64:]
        for at, term in enumerate(terms):
            low = lows[at]
            if group == 0:
                term[2 * GROUPS * HEAD :, :] = digits
            for half in range(2):
                block = low if half == 0 else 15 - low
                place = pl.ds(pl.multiple_of((block + 1) * BLOCK, BLOCK), BLOCK)
                lanes = slice(half * BLOCK, (half + 1) * BLOCK)
                term[group * HEAD : (group + 1) * HEAD, lanes] = (
                    dkt_ref[:, place] * SCALE
                ).astype(jnp.bfloat16)
                term[(GROUPS + group) * HEAD : (GROUPS + group + 1) * HEAD, lanes] = dvt_ref[
                    :, place
                ].astype(jnp.bfloat16)


def attention(me, count, docs, live_own, live_sib, q_own, q_sib, c_own, c_sib, chunks, interpret=False):
    vmem = pl.BlockSpec(memory_space=pltpu.VMEM)
    half_rows = jax.ShapeDtypeStruct((128, GROUPS * FOLD * HEAD), jnp.bfloat16)
    both_rows = jax.ShapeDtypeStruct((256, GROUPS * FOLD * HEAD), jnp.bfloat16)
    term = jax.ShapeDtypeStruct((TERM_ROWS, 2 * BLOCK), jnp.bfloat16)
    padded = 2048 + BLOCK
    most = 5
    return pl.pallas_call(
        attention_kernel,
        out_shape=(half_rows, half_rows, both_rows) + (term,) * 8,
        in_specs=[pl.BlockSpec(memory_space=pltpu.SMEM)] + [vmem] * 16,
        out_specs=(vmem,) * 11,
        scratch_shapes=[
            pltpu.VMEM((GROUPS, padded, HEAD), jnp.bfloat16),
            pltpu.VMEM((GROUPS, padded, 2 * HEAD), jnp.bfloat16),
            pltpu.VMEM((ROWS, most * TILE), jnp.float32),
            pltpu.VMEM((ROWS, most * TILE), jnp.bfloat16),
            pltpu.VMEM((ROWS, HEAD), jnp.bfloat16),
            pltpu.VMEM((ROWS, HEAD), jnp.bfloat16),
            pltpu.VMEM((HEAD, ROWS), jnp.bfloat16),
            pltpu.VMEM((HEAD, ROWS), jnp.bfloat16),
            pltpu.VMEM((ROWS, HEAD), jnp.float32),
            pltpu.VMEM((ROWS, 2 * HEAD), jnp.float32),
            pltpu.VMEM((ROWS, HEAD), jnp.float32),
            pltpu.VMEM((HEAD, padded), jnp.float32),
            pltpu.VMEM((HEAD, padded), jnp.float32),
        ],
        compiler_params=pltpu.CompilerParams(vmem_limit_bytes=28 * 1024 * 1024),
        cost_estimate=pl.CostEstimate(
            flops=6_000_000_000, bytes_accessed=8_000_000, transcendentals=4_000_000
        ),
        interpret=interpret,
    )(me, count, docs, live_own, live_sib, q_own, q_sib, c_own, c_sib, *chunks)


def closing_kernel(me_ref, *refs):
    terms, (kept, sent, ratio) = refs[:4], refs[4:]
    total = sum(term[...].astype(jnp.float32) for term in terms)
    width = 2 * GROUPS * HEAD
    digits = total[width : width + 8, :HEAD]
    count = digits[0:1] + DIGIT * (digits[1:2] + DIGIT * digits[2:3])
    ratio_row = 32768.0 / count
    ratio[...] = jnp.broadcast_to(ratio_row, (8, HEAD))
    rows = (total[:width] * ratio_row[:, :1]).T
    outer = jnp.concatenate([rows[:64], rows[192:]], axis=0).astype(jnp.bfloat16)
    inner = rows[64:192].astype(jnp.bfloat16)
    first = (me_ref[0] & 1) == 0
    kept[...] = jnp.where(first, outer, inner)
    sent[...] = jnp.where(first, inner, outer)


def closing(me, terms):
    vmem = pl.BlockSpec(memory_space=pltpu.VMEM)
    rows = jax.ShapeDtypeStruct((BLOCK, 2 * GROUPS * HEAD), jnp.bfloat16)
    return pl.pallas_call(
        closing_kernel,
        out_shape=(rows, rows, jax.ShapeDtypeStruct((8, HEAD), jnp.float32)),
        in_specs=[pl.BlockSpec(memory_space=pltpu.SMEM)] + [vmem] * 4,
        out_specs=(vmem,) * 3,
        compiler_params=pltpu.CompilerParams(vmem_limit_bytes=8 * 1024 * 1024),
        cost_estimate=pl.CostEstimate(flops=1_000_000, bytes_accessed=1_000_000, transcendentals=0),
    )(me, *terms)


def scale_kernel(me_ref, ratio, own, got, out):
    at = pl.program_id(0)
    mine = (at >> 1) == (me_ref[0] & 1)
    columns = pl.ds(pl.multiple_of((at & 1) * 1024, 1024), 1024)
    factor = ratio[0:1, 0:1]

    @pl.when(mine)
    def _():
        out[...] = (own[:, columns].astype(jnp.float32) * factor).astype(jnp.bfloat16)

    @pl.when(jnp.logical_not(mine))
    def _():
        out[...] = (got[BLOCK:, columns].astype(jnp.float32) * factor).astype(jnp.bfloat16)


def scaled(me, ratio, own, got):
    vmem = pl.BlockSpec(memory_space=pltpu.VMEM)
    return pl.pallas_call(
        scale_kernel,
        grid=(4,),
        out_shape=jax.ShapeDtypeStruct((BLOCK, 4096), jnp.bfloat16),
        in_specs=[pl.BlockSpec(memory_space=pltpu.SMEM)] + [vmem] * 3,
        out_specs=pl.BlockSpec((BLOCK, 1024), lambda i: (0, i)),
        compiler_params=pltpu.CompilerParams(vmem_limit_bytes=8 * 1024 * 1024),
        cost_estimate=pl.CostEstimate(flops=1_000_000, bytes_accessed=2_000_000, transcendentals=0),
    )(me, ratio, own, got)


def join_kernel(me_ref, kept, got, keys, values):
    first = (me_ref[0] & 1) == 0
    width = GROUPS * HEAD
    for at, out in enumerate((keys, values)):
        columns = slice(at * width, (at + 1) * width)
        own, other = kept[:, columns], got[:, columns]
        out[:, :width] = jnp.where(first, own, other)
        out[:, width:] = jnp.where(first, other, own)


def joined(me, kept, got):
    vmem = pl.BlockSpec(memory_space=pltpu.VMEM)
    whole = pl.BlockSpec((BLOCK, 2 * GROUPS * HEAD), lambda i: (0, 0))
    rows = jax.ShapeDtypeStruct((BLOCK, 2 * GROUPS * HEAD), jnp.bfloat16)
    return pl.pallas_call(
        join_kernel,
        grid=(1,),
        out_shape=(rows, rows),
        in_specs=[pl.BlockSpec(memory_space=pltpu.SMEM)] + [vmem] * 2,
        out_specs=(whole, whole),
        compiler_params=pltpu.CompilerParams(vmem_limit_bytes=4 * 1024 * 1024),
        cost_estimate=pl.CostEstimate(flops=100_000, bytes_accessed=500_000, transcendentals=0),
    )(me, kept, got)


def on_device(queries, keys, values, cotangent, live, docs):
    me = lax.axis_index("ctx")
    core = me % 2

    def move(shift):
        return [(i, (i + shift) % 16) for i in range(16)]

    def swap(bit):
        return [(i, i ^ bit) for i in range(16)]

    def to_right(a):
        return lax.ppermute(a, "ctx", move(4))

    def to_left(a):
        return lax.ppermute(a, "ctx", move(-4))

    def to_side(a):
        return lax.ppermute(a, "ctx", swap(2))

    def to_core(a):
        return lax.ppermute(a, "ctx", swap(1))

    kv_width = GROUPS * HEAD
    q_width = GROUPS * FOLD * HEAD
    keys_got, values_got = to_core(keys[0]), to_core(values[0])
    q_got, c_got = to_core(queries[0]), to_core(cotangent[0])

    def groups(a, b):
        chosen = [jnp.where(core == 0, x[:, :kv_width], x[:, kv_width:]) for x in (a, b)]
        return jnp.concatenate(chosen, axis=1)

    kv_keep, kv_got = groups(keys[0], values[0]), groups(keys_got, values_got)
    first = jnp.where(core == 0, kv_keep, kv_got)
    second = jnp.where(core == 0, kv_got, kv_keep)
    mine = jnp.concatenate([first[:64], second[:64], second[64:], first[64:]], axis=0)

    live_got = to_core(live)
    count = live + live_got
    for bit in (1, 2):
        count = count + lax.ppermute(count, "dp", swap(bit))

    from_left = to_right(mine)
    from_right = to_left(mine)
    beside = to_side(mine)
    beside, from_left, from_right, count = lax.optimization_barrier(
        (beside, from_left, from_right, count)
    )
    beside_left = to_right(beside)
    beside_right = to_left(beside)
    opposite = to_right(from_left)
    beside_opposite = to_left(beside_right)
    count = count + lax.ppermute(count, "dp", swap(8))
    count, _, _ = lax.optimization_barrier((count, beside_left, beside_right))
    count = count + lax.ppermute(count, "dp", swap(6))
    chunks = (
        mine,
        beside,
        from_right,
        beside_right,
        from_left,
        beside_left,
        opposite,
        beside_opposite,
    )

    device = me.reshape(1).astype(jnp.int32)
    results = attention(
        device,
        count,
        docs,
        live,
        live_got,
        queries[0],
        q_got,
        cotangent[0],
        c_got,
        chunks,
    )
    o_own, dq_own, sib_out = results[:3]
    t_mine, t_beside, t_right, t_beside_right, t_left, t_beside_left, t_opp, t_beside_opp = (
        results[3:]
    )

    def add(*terms):
        return sum(t.astype(jnp.float32) for t in terms).astype(jnp.bfloat16)

    opp_via_right = to_right(t_opp)
    opp_via_left = to_left(t_beside_opp)
    got_beside_1 = to_right(t_beside_right)
    right_sum, left_sum = add(t_right, opp_via_right), add(t_beside_left, opp_via_left)
    got_mine_2 = to_right(right_sum)
    got_beside_2 = to_left(left_sum)
    got_mine_1 = to_left(t_left)
    beside_sum = add(t_beside, got_beside_1, got_beside_2)
    sib_out, *_ = lax.optimization_barrier((sib_out, opp_via_left, opp_via_right))
    sib_got = to_core(sib_out)
    got_side = to_side(beside_sum)
    def join(own, got, width):
        low = jnp.where(core == 0, own, got)
        high = jnp.where(core == 0, got, own)
        return jnp.concatenate([low, high], axis=1)

    attended = join(o_own, sib_got[:BLOCK], q_width)[None]
    t_mine, attended = lax.optimization_barrier((t_mine, attended))
    kept, sent, ratio = closing(device, (t_mine, got_mine_1, got_mine_2, got_side))
    got = to_core(sent)

    grad_queries = scaled(device, ratio, dq_own, sib_got)[None]
    got, grad_queries = lax.optimization_barrier((got, grad_queries))
    key_gradient, value_gradient = joined(device, kept, got)
    return attended, grad_queries, key_gradient[None], value_gradient[None]


def solution(mesh):
    rows = P("dp", "ctx", None)
    return jax.shard_map(
        on_device,
        mesh=mesh,
        in_specs=(rows, rows, rows, rows, P("dp", "ctx"), P("dp", None)),
        out_specs=(rows, rows, rows, rows),
        check_vma=False,
    )
```
